512 devices in a mesh: frames: 32 (over y, x, core), atoms: 16 (over z).
Axes of the slice: x: 4, y: 4, z: 16, core: 2. Of those that a mesh axis runs over, the one named last changes fastest.
Arguments:
- frames: float32 [2048, 3, 6144], P('frames', None, 'atoms'), may hold values from -45 to 45, as said below
- reference_structure: float32 [3, 6144], P(None, 'atoms'), may hold values from -15 to 15
Outputs:
- covariance: float32 [3, 6144, 3, 6144], P(None, 'frames', None, 'atoms')
- mean_structure: float32 [3, 6144], P(None, 'atoms')
The draws below stay inside these ranges and needn't reach their ends.
Inputs may be any that keep to these rules, and one draw needn't show every extreme that they name: `frames`: every frame, once centered, has a cross-covariance with the centered reference_structure of positive determinant whose singular values lie within a factor of 20 of one another.
All inputs are finite; a program needn't handle non-finite values.
Results may differ from the reference program's by a relative error of at most 0.0003.
Values may be sent and summed in bfloat16 or wider, within the bound.
A program may use at most 64 MiB of HBM per device.

```python
import jax
import jax.numpy as jnp
from jax import lax

ATOMS = 6144
ITERS = 2
POLAR = 8
FRAMES = 2048


def base_structure(key):
    points = jax.random.normal(jax.random.fold_in(key, 101), (3, ATOMS), jnp.float32)
    spread = jnp.array([3.0, 3.0, 3.0], jnp.float32)
    return jnp.clip(points * spread[:, None], -12.0, 12.0)


def unit_vector(key, salt):
    raw = jax.random.normal(jax.random.fold_in(key, salt), (3,), jnp.float32)
    return raw / jnp.sqrt(jnp.sum(raw * raw) + 1e-12)


def hinge_setup(key):
    base = base_structure(key)
    first_axis = unit_vector(key, 111)
    other_axis = unit_vector(key, 112)
    other_axis = other_axis - jnp.sum(other_axis * first_axis) * first_axis
    other_axis = other_axis / jnp.sqrt(jnp.sum(other_axis * other_axis) + 1e-12)
    facing = unit_vector(key, 113)
    domain = (jnp.sum(facing[:, None] * base, axis=0) > 0.0).astype(jnp.float32)
    return (base, first_axis, other_axis, domain)


def axis_rotation(axis, angle):
    zero = jnp.zeros((), jnp.float32)
    generator = jnp.stack([jnp.stack([zero, -axis[2], axis[1]]), jnp.stack([axis[2], zero, -axis[0]]), jnp.stack([-axis[1], axis[0], zero])])
    generator_sq = jnp.dot(generator, generator, precision=jax.lax.Precision.HIGHEST)
    return jnp.eye(3, dtype=jnp.float32)[None] + jnp.sin(angle)[:, None, None] * generator[None] + (1.0 - jnp.cos(angle))[:, None, None] * generator_sq[None]


def hinged(base, domain, turns):
    rotated = jnp.einsum('nij,ja->nia', turns, base, precision=jax.lax.Precision.HIGHEST)
    return base[None] + domain[None, None, :] * (rotated - base[None])


def draw_reference_structure(key, part):
    base, first_axis, other_axis, domain = hinge_setup(key)
    magnitude = jax.random.uniform(jax.random.fold_in(key, 203), (1,), jnp.float32, 0.6, 0.9)
    flip_sign = jnp.where(jax.random.uniform(jax.random.fold_in(key, 204), (1,), jnp.float32) < 0.5, -1.0, 1.0)
    shaped = hinged(base, domain, axis_rotation(other_axis, magnitude * flip_sign))[0]
    jitter = jnp.clip(0.5 * jax.random.normal(jax.random.fold_in(key, 202), (3, ATOMS), jnp.float32), -3.0, 3.0)
    return jnp.clip(shaped + jitter, -15.0, 15.0)


def draw_frames(key, part):
    base, first_axis, other_axis, domain = hinge_setup(key)
    swings = jnp.clip(0.7 * jax.random.normal(jax.random.fold_in(key, 309), (FRAMES,), jnp.float32), -1.2, 1.2)
    shaped = hinged(base, domain, axis_rotation(first_axis, swings))
    atom_spread = jnp.exp(jax.random.uniform(jax.random.fold_in(key, 303), (ATOMS,), jnp.float32, jnp.log(0.3), jnp.log(1.5)))
    noise = jax.random.normal(jax.random.fold_in(key, 304), (FRAMES, 3, ATOMS), jnp.float32) * atom_spread[None, None, :]
    noise = jnp.clip(noise, -6.0, 6.0)
    quats = jax.random.normal(jax.random.fold_in(key, 307), (FRAMES, 4), jnp.float32)
    quats = quats / jnp.sqrt(jnp.sum(quats * quats, axis=1, keepdims=True) + 1e-12)
    a, b, c, d = (quats[:, 0], quats[:, 1], quats[:, 2], quats[:, 3])
    rotation = jnp.stack([jnp.stack([1 - 2 * (c * c + d * d), 2 * (b * c - d * a), 2 * (b * d + c * a)], axis=1), jnp.stack([2 * (b * c + d * a), 1 - 2 * (b * b + d * d), 2 * (c * d - b * a)], axis=1), jnp.stack([2 * (b * d - c * a), 2 * (c * d + b * a), 1 - 2 * (b * b + c * c)], axis=1)], axis=1)
    moved = jnp.einsum('fij,fja->fia', rotation, shaped + noise, precision=jax.lax.Precision.HIGHEST)
    offset = jnp.clip(5.0 * jax.random.normal(jax.random.fold_in(key, 308), (FRAMES, 3, 1), jnp.float32), -10.0, 10.0)
    return jnp.clip(moved + offset, -45.0, 45.0)


def setup_inputs(seed: int = 0) -> dict:
    seeds = jax.random.split(jax.random.key(seed), 3)
    return {
        "frames": draw_frames(jax.random.fold_in(seeds[2], 71), 0),
        "reference_structure": draw_reference_structure(jax.random.fold_in(seeds[2], 71), 0),
    }


def polar_factor(cross):
    factor = jnp.sqrt(3.0 / lax.optimization_barrier(jnp.sum(cross * cross, axis=(0, 1))))
    matrix = cross * factor[None, None, :]
    for turn in range(POLAR):
        entries = [[matrix[i, j] for j in range(3)] for i in range(3)]
        cofactor = [[entries[(i + 1) % 3][(j + 1) % 3] * entries[(i + 2) % 3][(j + 2) % 3] - entries[(i + 1) % 3][(j + 2) % 3] * entries[(i + 2) % 3][(j + 1) % 3] for j in range(3)] for i in range(3)]
        determinant = entries[0][0] * cofactor[0][0] + entries[0][1] * cofactor[0][1] + entries[0][2] * cofactor[0][2]
        inverse = jnp.stack([jnp.stack(cofactor[i]) for i in range(3)]) / determinant[None, None, :]
        matrix = 0.5 * (matrix + inverse)
    return matrix

def reference(frames, reference_structure):
    highest = lax.Precision.HIGHEST
    mean_now = reference_structure
    for iteration in range(ITERS):
        centroid = lax.optimization_barrier(jnp.sum(frames, axis=2)) / ATOMS
        shifted = frames - centroid[:, :, None]
        cross = jnp.einsum('fca,da->cdf', shifted, mean_now, precision=highest)
        rotation = polar_factor(cross)
        aligned = jnp.einsum('cdf,fca->fda', rotation, shifted, precision=highest)
        mean_now = lax.optimization_barrier(jnp.sum(aligned, axis=0)) / FRAMES
    deviation = (aligned - mean_now[None]).astype(jnp.bfloat16).reshape(FRAMES, 3 * ATOMS)
    product = lax.dot_general(deviation, deviation, (((0,), (0,)), ((), ())), preferred_element_type=jnp.float32)
    covariance = (product / FRAMES).reshape(3, ATOMS, 3, ATOMS)
    return (covariance, mean_now)
```

```python
import jax
import jax.numpy as jnp
from jax import lax
from jax.experimental import pallas as pl
from jax.experimental.pallas import tpu as pltpu
from jax.sharding import PartitionSpec as P

ATOMS = 6144
FRAMES = 2048
POLAR = 8
F = 64
A = 384
W = 3 * A
NZ = 16
NP = 32
H = F // 2
MESH = pl.DeviceIdType.MESH
HIGHEST = lax.Precision.HIGHEST


def polar_factor(cross):
    square = sum(cross[i][j] * cross[i][j] for i in range(3) for j in range(3))
    factor = jnp.sqrt(3.0 / square)
    flat = tuple(cross[i][j] * factor for i in range(3) for j in range(3))

    def turn(_, flat):
        e = [flat[0:3], flat[3:6], flat[6:9]]
        cof = [
            [
                e[(i + 1) % 3][(j + 1) % 3] * e[(i + 2) % 3][(j + 2) % 3]
                - e[(i + 1) % 3][(j + 2) % 3] * e[(i + 2) % 3][(j + 1) % 3]
                for j in range(3)
            ]
            for i in range(3)
        ]
        det = e[0][0] * cof[0][0] + e[0][1] * cof[0][1] + e[0][2] * cof[0][2]
        half = 0.5 / det
        return tuple(0.5 * e[i][j] + cof[i][j] * half for i in range(3) for j in range(3))

    flat = lax.fori_loop(0, POLAR, turn, flat)
    return [flat[0:3], flat[3:6], flat[6:9]]


def kernel(
    frames_ref, ref_ref, cov_ref, mean_ref,
    fa, aug, w, tile, rt, al, zbuf, pbuf, col, row, acc,
    z_send, z_recv, p_send, p_recv,
    a_send, a_recv, b_send, b_recv, cs_send, cs_recv,
    swap_send, swap_recv, r_send, r_recv, rs_send, rs_recv,
):
    me = lax.axis_index("frames")
    z = lax.axis_index("atoms")
    c = me // 2
    k = me % 2
    y = c // 4
    x = c % 4
    pa = x + k * (y - x)
    pb = y + k * (x - y)
    partner = (z * 2 + k, c)
    sibling = (c * 2 + 1 - k, z)

    barrier = pltpu.get_barrier_semaphore()

    def greet_z(j, _):
        pl.semaphore_signal(barrier, inc=1, device_id=(me, (z + j) % NZ), device_id_type=MESH)
        return 0

    def greet_p(j, _):
        pl.semaphore_signal(barrier, inc=1, device_id=((me + j) % NP, z), device_id_type=MESH)
        return 0

    lax.fori_loop(1, NZ, greet_z, 0)
    lax.fori_loop(1, NP, greet_p, 0)

    @pl.when(c != z)
    def _():
        pl.semaphore_signal(barrier, inc=1, device_id=partner, device_id_type=MESH)

    fa[0:F, :] = frames_ref[:, 0, :]
    fa[F : 2 * F, :] = frames_ref[:, 2, :]
    fa[2 * F : 3 * F, :] = frames_ref[:, 1, :]
    fa[3 * F : 4 * F, :] = jnp.ones((F, A), jnp.float32)
    aug[...] = jnp.zeros((16, A), jnp.float32)
    aug[3:4, :] = jnp.ones((1, A), jnp.float32)
    aug[15:16, :] = jnp.ones((1, A), jnp.float32)
    w[...] = jnp.zeros((8, 4 * F), jnp.float32)
    rt[...] = jnp.zeros((16, 2 * F), jnp.float32)
    acc[...] = jnp.zeros((3, 256, W), jnp.float32)
    low = lax.broadcasted_iota(jnp.int32, (1, 2 * F), 1) < F

    def local_sums():
        nt = (((1,), (1,)), ((), ()))
        first = lax.dot_general(
            aug[0:8, :], fa[0 : 2 * F, :], nt, precision=HIGHEST, preferred_element_type=jnp.float32
        )
        second = lax.dot_general(
            aug[8:16, :], fa[2 * F : 4 * F, :], nt, precision=HIGHEST, preferred_element_type=jnp.float32
        )
        return first + second

    mean_now = ref_ref[...]
    for p in range(2):
        aug[0:3, :] = mean_now
        aug[12:15, :] = mean_now
        zbuf[p, z] = local_sums()
        if p == 0:
            pl.semaphore_wait(barrier, NZ + NP - 2 + jnp.where(c != z, 1, 0))

        def z_copy(j):
            return pltpu.make_async_remote_copy(
                zbuf.at[p, z], zbuf.at[p, z], z_send.at[p, j], z_recv.at[p, z],
                device_id=(me, (z + j) % NZ), device_id_type=MESH,
            )

        def z_start(j, _):
            z_copy(j).start()
            return 0

        def z_wait(j, _):
            other = (z + j) % NZ
            pltpu.make_async_remote_copy(
                zbuf.at[p, other], zbuf.at[p, other], z_send.at[p, j], z_recv.at[p, other],
                device_id=(me, other), device_id_type=MESH,
            ).wait_recv()
            return 0

        lax.fori_loop(1, NZ, z_start, 0)
        lax.fori_loop(1, NZ, z_wait, 0)
        total = zbuf[p, 0]
        for i in range(1, NZ):
            total = total + zbuf[p, i]
        tile[0:8, :] = total
        tile[8:16, :] = pltpu.roll(total, F, 1)
        centroid = [tile[r : r + 1, :] / ATOMS for r in (3, 7, 11)]
        cross = [
            [tile[4 * i + d : 4 * i + d + 1, :] - centroid[i] * tile[12 + d : 13 + d, :] for d in range(3)]
            for i in range(3)
        ]
        rotation = polar_factor(cross)
        for d in range(3):
            back = -(
                rotation[0][d] * centroid[0] + rotation[1][d] * centroid[1] + rotation[2][d] * centroid[2]
            )
            w[d : d + 1, 0 : 2 * F] = jnp.where(low, rotation[0][d], pltpu.roll(rotation[2][d], F, 1))
            w[d : d + 1, 2 * F : 4 * F] = jnp.where(low, rotation[1][d], pltpu.roll(back, F, 1))
        part = lax.dot_general(
            w[...], fa[...], (((1,), (0,)), ((), ())), precision=HIGHEST, preferred_element_type=jnp.float32
        )
        pbuf[p, me] = part[0:4, :]

        def p_start(j, _):
            pltpu.make_async_remote_copy(
                pbuf.at[p, me], pbuf.at[p, me], p_send.at[p, j], p_recv.at[p, me],
                device_id=((me + j) % NP, z), device_id_type=MESH,
            ).start()
            return 0

        def p_wait(j, _):
            other = (me + j) % NP
            pltpu.make_async_remote_copy(
                pbuf.at[p, other], pbuf.at[p, other], p_send.at[p, j], p_recv.at[p, other],
                device_id=(other, z), device_id_type=MESH,
            ).wait_recv()
            return 0

        lax.fori_loop(1, NP, p_start, 0)
        if p == 1:
            for i in range(3):
                for d in range(3):
                    rt[3 * i + d : 3 * i + d + 1, :] = rotation[i][d]
                rt[9 + i : 10 + i, :] = centroid[i]
            columns = jnp.transpose(rt[...])[0:F, :]
            shifted = [
                fa[at : at + F, :] - columns[:, 9 + i : 10 + i] for i, at in enumerate((0, 2 * F, F))
            ]
            for d in range(3):
                al[d] = sum(columns[:, 3 * i + d : 3 * i + d + 1] * shifted[i] for i in range(3))
        lax.fori_loop(1, NP, p_wait, 0)
        summed = pbuf[p, 0]
        for i in range(1, NP):
            summed = summed + pbuf[p, i]
        mean_now = summed[0:3, :] / FRAMES

    mean_ref[...] = mean_now
    for d in range(3):
        col[c, k, :, d * A : (d + 1) * A] = (al[d] - mean_now[d : d + 1, :]).astype(jnp.bfloat16)

    @pl.when(c == z)
    def _():
        row[z, k] = col[c, k]

    def copy(src, dst, send, recv, device):
        return pltpu.make_async_remote_copy(src, dst, send, recv, device_id=device, device_id_type=MESH)

    def swap(slot):
        return copy(col.at[c, k], row.at[slot, k], swap_send, swap_recv, partner)

    @pl.when(c != z)
    def _():
        swap(c).start()

    def chip(oa, ob):
        qa, qb = (pa + oa) % 4, (pb + ob) % 4
        return (qb + k * (qa - qb)) * 4 + qa + k * (qb - qa)

    def at(oa, ob):
        return (chip(oa, ob) * 2 + k, z)

    def part_of(slot, half):
        if half is None:
            return col.at[slot, k]
        return col.at[slot, k, half * H : (half + 1) * H]

    HALF = (None, None, 0, 1)
    TOWARD = (1, 3, 1, 3)

    def a_copy(kind, slot):
        r = part_of(slot, HALF[kind])
        return copy(r, r, a_send.at[kind], a_recv.at[kind], at(TOWARD[kind], 0))

    def b_copy(oa, kind, slot):
        r = part_of(slot, HALF[kind])
        return copy(r, r, b_send.at[oa, kind], b_recv.at[oa, kind], at(0, TOWARD[kind]))

    def col_sibling(slot, core):
        r = col.at[slot, core]
        return copy(r, r, cs_send.at[slot], cs_recv.at[slot], sibling)

    def have(oa):
        slot = chip(oa, 0)
        b_copy(oa, 0, slot).start()
        b_copy(oa, 1, slot).start()
        col_sibling(slot, k).start()

    def b_pass(oa):
        before, after = chip(oa, 3), chip(oa, 1)
        b_copy(oa, 0, before).wait_recv()
        b_copy(oa, 2, before).start()
        col_sibling(before, k).start()
        b_copy(oa, 1, after).wait_recv()
        b_copy(oa, 3, after).start()
        col_sibling(after, k).start()

    def b_end(oa):
        slot = chip(oa, 2)
        b_copy(oa, 2, slot).wait_recv()
        b_copy(oa, 3, slot).wait_recv()
        col_sibling(slot, k).start()

    right, left = (me, (z + 1) % NZ), (me, (z + NZ - 1) % NZ)

    def r_copy(way, step, h, slot):
        r = row.at[slot, k, h * H : (h + 1) * H]
        return copy(r, r, r_send.at[way, step, h], r_recv.at[way, step, h], right if way == 0 else left)

    def row_sibling(offset, core):
        r = row.at[(z + offset) % NZ, core]
        return copy(r, r, rs_send.at[offset], rs_recv.at[offset], sibling)

    def z_step(s, last=False):
        before, after = (z + NZ - s) % NZ, (z + s) % NZ
        for h in range(2):
            r_copy(0, s - 1, h, before).wait_recv()
            if not last or h == 0:
                r_copy(0, s, h, before).start()
            r_copy(1, s - 1, h, after).wait_recv()
            if not last or h == 1:
                r_copy(1, s, h, after).start()
        row_sibling(NZ - s, k).start()
        row_sibling(s, k).start()

    def accumulate(one, two):
        def component(d, _):
            lanes = pl.ds(pl.multiple_of(d * A + k * 128, 128), 256)
            lhs = jnp.concatenate(
                [row[one, 0, :, lanes], row[one, 1, :, lanes], row[two, 0, :, lanes], row[two, 1, :, lanes]], axis=0
            )
            rhs = jnp.concatenate([col[one, 0], col[one, 1], col[two, 0], col[two, 1]], axis=0)
            acc[d] += lax.dot_general(
                lhs, rhs, (((0,), (0,)), ((), ())), preferred_element_type=jnp.float32
            )
            return 0

        lax.fori_loop(0, 3, component, 0)

    def z_compute(s):
        row_sibling(s, 1 - k).wait_recv()
        row_sibling(NZ - s, 1 - k).wait_recv()
        accumulate((z + NZ - s) % NZ, (z + s) % NZ)

    a_copy(0, c).start()
    a_copy(1, c).start()
    have(0)
    a_copy(0, chip(3, 0)).wait_recv()
    a_copy(2, chip(3, 0)).start()
    have(3)
    a_copy(1, chip(1, 0)).wait_recv()
    a_copy(3, chip(1, 0)).start()
    have(1)

    @pl.when(c != z)
    def _():
        swap(z).wait_recv()

    for h in range(2):
        r_copy(0, 0, h, z).start()
        r_copy(1, 0, h, z).start()
    row_sibling(0, k).start()
    b_pass(0)
    a_copy(2, chip(2, 0)).wait_recv()
    a_copy(3, chip(2, 0)).wait_recv()
    have(2)
    b_pass(3)
    z_step(1)
    b_pass(1)
    b_pass(2)
    z_step(2)
    for oa in (0, 3, 1, 2):
        b_end(oa)

    def col_wait(q, _):
        col_sibling(q, 1 - k).wait_recv()
        return 0

    def compute(s, _):
        z_compute(s)
        return 0

    def middle(s, _):
        z_step(s)
        z_compute(s - 1)
        return 0

    z_step(3)
    lax.fori_loop(0, NZ, col_wait, 0)
    lax.fori_loop(1, 3, compute, 0)
    lax.fori_loop(4, 7, middle, 0)
    z_step(7, last=True)
    lax.fori_loop(6, 8, compute, 0)
    far = (z + NZ // 2) % NZ
    r_copy(0, 7, 0, far).wait_recv()
    r_copy(1, 7, 1, far).wait_recv()
    row_sibling(NZ // 2, k).start()
    row_sibling(0, 1 - k).wait_recv()
    row_sibling(NZ // 2, 1 - k).wait_recv()
    accumulate(z, far)
    for d in range(3):
        cov_ref[d] = acc[d, pl.ds(pl.multiple_of(k * F, F), 192), :] * (1.0 / FRAMES)

    def a_sent(j, _):
        for p in range(2):
            copy(zbuf.at[p, z], zbuf.at[p, z], z_send.at[p, j], z_recv.at[p, z], (me, (z + j) % NZ)).wait_send()
        return 0

    def p_sent(j, _):
        for p in range(2):
            copy(pbuf.at[p, me], pbuf.at[p, me], p_send.at[p, j], p_recv.at[p, me], ((me + j) % NP, z)).wait_send()
        return 0

    def slot_sent(q, _):
        col_sibling(q, k).wait_send()
        row_sibling(q, k).wait_send()
        return 0

    def b_sent(oa, _):
        for kind in range(4):
            b_copy(oa, kind, c).wait_send()
        return 0

    def r_sent(s, _):
        for way in range(2):
            for h in range(2):
                r_copy(way, s, h, z).wait_send()
        return 0

    lax.fori_loop(1, NZ, a_sent, 0)
    lax.fori_loop(1, NP, p_sent, 0)
    lax.fori_loop(0, NZ, slot_sent, 0)
    for kind in range(4):
        a_copy(kind, c).wait_send()
    lax.fori_loop(0, 4, b_sent, 0)
    lax.fori_loop(0, NZ // 2 - 1, r_sent, 0)
    r_copy(0, 7, 0, z).wait_send()
    r_copy(1, 7, 1, z).wait_send()

    @pl.when(c != z)
    def _():
        swap(c).wait_send()


def body(frames, reference_structure):
    dma = pltpu.SemaphoreType.DMA
    vmem = pl.BlockSpec(memory_space=pltpu.VMEM)
    covariance, mean = pl.pallas_call(
        kernel,
        out_shape=(
            jax.ShapeDtypeStruct((3, A // 2, W), jnp.float32),
            jax.ShapeDtypeStruct((3, A), jnp.float32),
        ),
        in_specs=[vmem, vmem],
        out_specs=(vmem, vmem),
        scratch_shapes=[
            pltpu.VMEM((4 * F, A), jnp.float32),
            pltpu.VMEM((16, A), jnp.float32),
            pltpu.VMEM((8, 4 * F), jnp.float32),
            pltpu.VMEM((16, 2 * F), jnp.float32),
            pltpu.VMEM((16, 2 * F), jnp.float32),
            pltpu.VMEM((3, F, A), jnp.float32),
            pltpu.VMEM((2, NZ, 8, 2 * F), jnp.float32),
            pltpu.VMEM((2, NP, 4, A), jnp.float32),
            pltpu.VMEM((NZ, 2, F, W), jnp.bfloat16),
            pltpu.VMEM((NZ, 2, F, W), jnp.bfloat16),
            pltpu.VMEM((3, 256, W), jnp.float32),
            dma((2, NZ)), dma((2, NZ)), dma((2, NP)), dma((2, NP)),
            dma((4,)), dma((4,)), dma((4, 4)), dma((4, 4)), dma((NZ,)), dma((NZ,)),
            dma, dma, dma((2, 8, 2)), dma((2, 8, 2)), dma((NZ,)), dma((NZ,)),
        ],
        compiler_params=pltpu.CompilerParams(
            collective_id=0, has_side_effects=True, vmem_limit_bytes=44 * 1024 * 1024
        ),
        cost_estimate=pl.CostEstimate(flops=3_000_000_000, bytes_accessed=8_000_000, transcendentals=0),
    )(frames, reference_structure)
    return covariance.reshape(3, A // 2, 3, A), mean


def solution(mesh):
    return jax.shard_map(
        body,
        mesh=mesh,
        in_specs=(P("frames", None, "atoms"), P(None, "atoms")),
        out_specs=(P(None, "frames", None, "atoms"), P(None, "atoms")),
        check_vma=False,
    )
```

```python
import jax
import jax.numpy as jnp
from jax import lax
from jax.experimental import pallas as pl
from jax.experimental.pallas import tpu as pltpu
from jax.sharding import PartitionSpec as P

ATOMS = 6144
FRAMES = 2048
POLAR = 8
F = 64
A = 384
W = 3 * A
NZ = 16
NP = 32
H = F // 2
CH = 4
Q = F // CH
MESH = pl.DeviceIdType.MESH
HIGHEST = lax.Precision.HIGHEST


def polar_factor(cross):
    square = sum(cross[i][j] * cross[i][j] for i in range(3) for j in range(3))
    factor = jnp.sqrt(3.0 / square)
    flat = tuple(cross[i][j] * factor for i in range(3) for j in range(3))

    def turn(_, flat):
        e = [flat[0:3], flat[3:6], flat[6:9]]
        cof = [
            [
                e[(i + 1) % 3][(j + 1) % 3] * e[(i + 2) % 3][(j + 2) % 3]
                - e[(i + 1) % 3][(j + 2) % 3] * e[(i + 2) % 3][(j + 1) % 3]
                for j in range(3)
            ]
            for i in range(3)
        ]
        det = e[0][0] * cof[0][0] + e[0][1] * cof[0][1] + e[0][2] * cof[0][2]
        half = 0.5 / det
        return tuple(0.5 * e[i][j] + cof[i][j] * half for i in range(3) for j in range(3))

    flat = lax.fori_loop(0, POLAR, turn, flat)
    return [flat[0:3], flat[3:6], flat[6:9]]


def kernel(
    frames_ref, ref_ref, cov_ref, mean_ref,
    fa, aug, w, tile, rt, al, zbuf, pbuf, mid, col, row, acc,
    z_send, z_recv, p_send, p_recv,
    a_send, a_recv, b_send, b_recv, cs_send, cs_recv,
    l_send, l_recv, r_send, r_recv, rs_send, rs_recv,
):
    me = lax.axis_index("frames")
    z = lax.axis_index("atoms")
    c = me // 2
    k = me % 2
    y = c // 4
    x = c % 4
    pa = x + k * (y - x)
    pb = y + k * (x - y)
    sibling = (c * 2 + 1 - k, z)

    def copy(src, dst, send, recv, device):
        return pltpu.make_async_remote_copy(src, dst, send, recv, device_id=device, device_id_type=MESH)

    def z_other(i):
        return (z + 8 + ((i + 1) // 2) * (2 * (i % 2) - 1)) % NZ

    def p_other(i):
        return (((y + i // 8 + 2) % 4) * 4 + (x + i // 2 + 2) % 4) * 2 + (k + i) % 2

    def over_z(act):
        def turn(i, _):
            act(i, z_other(i))
            return 0

        lax.fori_loop(0, NZ - 1, turn, 0)

    def over_p(act):
        def turn(i, _):
            act(i, p_other(i))
            return 0

        lax.fori_loop(0, 20, turn, 0)
        lax.fori_loop(21, NP, turn, 0)

    barrier = pltpu.get_barrier_semaphore()
    over_z(lambda i, o: pl.semaphore_signal(barrier, inc=1, device_id=(me, o), device_id_type=MESH))
    over_p(lambda i, o: pl.semaphore_signal(barrier, inc=1, device_id=(o, z), device_id_type=MESH))

    fa[0:F, :] = frames_ref[0]
    fa[F : 2 * F, :] = frames_ref[2]
    fa[2 * F : 3 * F, :] = frames_ref[1]
    fa[3 * F : 4 * F, :] = jnp.ones((F, A), jnp.float32)
    aug[...] = jnp.zeros((16, A), jnp.float32)
    aug[3:4, :] = jnp.ones((1, A), jnp.float32)
    aug[15:16, :] = jnp.ones((1, A), jnp.float32)
    w[...] = jnp.zeros((8, 4 * F), jnp.float32)
    rt[...] = jnp.zeros((16, 2 * F), jnp.float32)
    acc[...] = jnp.zeros((3, 256, W), jnp.float32)
    low = lax.broadcasted_iota(jnp.int32, (1, 2 * F), 1) < F

    def local_sums():
        nt = (((1,), (1,)), ((), ()))
        first = lax.dot_general(
            aug[0:8, :], fa[0 : 2 * F, :], nt, precision=HIGHEST, preferred_element_type=jnp.float32
        )
        second = lax.dot_general(
            aug[8:16, :], fa[2 * F : 4 * F, :], nt, precision=HIGHEST, preferred_element_type=jnp.float32
        )
        return first + second

    mean_now = ref_ref[...]
    for p in range(2):
        aug[0:3, :] = mean_now
        aug[12:15, :] = mean_now
        zbuf[p, z] = local_sums()
        if p == 0:
            pl.semaphore_wait(barrier, NZ + NP - 2)

        def z_copy(i, o, slot):
            return copy(zbuf.at[p, slot], zbuf.at[p, slot], z_send.at[p, i], z_recv.at[p, slot], (me, o))

        over_z(lambda i, o: z_copy(i, o, z).start())
        over_z(lambda i, o: z_copy(i, o, o).wait_recv())
        total = zbuf[p, 0]
        for i in range(1, NZ):
            total = total + zbuf[p, i]
        tile[0:8, :] = total
        tile[8:16, :] = pltpu.roll(total, F, 1)
        centroid = [tile[r : r + 1, :] / ATOMS for r in (3, 7, 11)]
        cross = [
            [tile[4 * i + d : 4 * i + d + 1, :] - centroid[i] * tile[12 + d : 13 + d, :] for d in range(3)]
            for i in range(3)
        ]
        rotation = polar_factor(cross)
        for d in range(3):
            back = -(
                rotation[0][d] * centroid[0] + rotation[1][d] * centroid[1] + rotation[2][d] * centroid[2]
            )
            w[d : d + 1, 0 : 2 * F] = jnp.where(low, rotation[0][d], pltpu.roll(rotation[2][d], F, 1))
            w[d : d + 1, 2 * F : 4 * F] = jnp.where(low, rotation[1][d], pltpu.roll(back, F, 1))
        part = lax.dot_general(
            w[...], fa[...], (((1,), (0,)), ((), ())), precision=HIGHEST, preferred_element_type=jnp.float32
        )
        pbuf[p, me] = part[0:4, :]

        def p_copy(i, o, slot):
            return copy(pbuf.at[p, slot], pbuf.at[p, slot], p_send.at[p, i], p_recv.at[p, slot], (o, z))

        over_p(lambda i, o: p_copy(i, o, me).start())
        if p == 1:
            for i in range(3):
                for d in range(3):
                    rt[3 * i + d : 3 * i + d + 1, :] = rotation[i][d]
                rt[9 + i : 10 + i, :] = centroid[i]
            columns = jnp.transpose(rt[...])[0:F, :]
            shifted = [frames_ref[i] - columns[:, 9 + i : 10 + i] for i in range(3)]
            for d in range(3):
                al[d] = sum(columns[:, 3 * i + d : 3 * i + d + 1] * shifted[i] for i in range(3))
        over_p(lambda i, o: p_copy(i, o, o).wait_recv())
        summed = pbuf[p, 0]
        for i in range(1, NP):
            summed = summed + pbuf[p, i]
        mean_now = summed[0:3, :] / FRAMES

    mean_ref[...] = mean_now
    for d in range(3):
        col[c, k, :, d * A : (d + 1) * A] = (al[d] - mean_now[d : d + 1, :]).astype(jnp.bfloat16)

    leg_z = (5 * z + c) % NZ
    leg_p = (13 * (z + NZ - c)) % NZ
    seed = (z + 5 * NZ - 5 * c) % NZ

    def leg_1(n):
        rows = pl.ds(n * Q, Q)
        return copy(col.at[c, k, rows], mid.at[rows], l_send.at[0, n], l_recv.at[0, n], (me, leg_z))

    def leg_2(n, slot):
        rows = pl.ds(n * Q, Q)
        return copy(mid.at[rows], row.at[slot, k, rows], l_send.at[1, n], l_recv.at[1, n], (leg_p * 2 + k, z))

    @pl.when(leg_z != z)
    def _():
        for n in range(CH):
            leg_1(n).start()

    @pl.when(leg_z == z)
    def _():
        mid[...] = col[c, k]

    def chip(oa, ob):
        qa, qb = (pa + oa) % 4, (pb + ob) % 4
        return (qb + k * (qa - qb)) * 4 + qa + k * (qb - qa)

    def at(oa, ob):
        return (chip(oa, ob) * 2 + k, z)

    def part_of(slot, half):
        if half is None:
            return col.at[slot, k]
        return col.at[slot, k, half * H : (half + 1) * H]

    HALF = (None, None, 0, 1)
    TOWARD = (1, 3, 1, 3)

    def a_copy(kind, slot):
        r = part_of(slot, HALF[kind])
        return copy(r, r, a_send.at[kind], a_recv.at[kind], at(TOWARD[kind], 0))

    def b_copy(oa, kind, slot):
        r = part_of(slot, HALF[kind])
        return copy(r, r, b_send.at[oa, kind], b_recv.at[oa, kind], at(0, TOWARD[kind]))

    def col_sibling(slot, core):
        r = col.at[slot, core]
        return copy(r, r, cs_send.at[slot], cs_recv.at[slot], sibling)

    def have(oa):
        slot = chip(oa, 0)
        b_copy(oa, 0, slot).start()
        b_copy(oa, 1, slot).start()
        col_sibling(slot, k).start()

    def b_pass(oa):
        before, after = chip(oa, 3), chip(oa, 1)
        b_copy(oa, 0, before).wait_recv()
        b_copy(oa, 2, before).start()
        col_sibling(before, k).start()
        b_copy(oa, 1, after).wait_recv()
        b_copy(oa, 3, after).start()
        col_sibling(after, k).start()

    def b_end(oa):
        slot = chip(oa, 2)
        b_copy(oa, 2, slot).wait_recv()
        b_copy(oa, 3, slot).wait_recv()
        col_sibling(slot, k).start()

    right, left = (me, (z + 1) % NZ), (me, (z + NZ - 1) % NZ)

    def off(offset):
        return (seed + offset) % NZ

    def r_copy(way, step, h, slot):
        r = row.at[slot, k, h * Q : (h + 1) * Q]
        return copy(r, r, r_send.at[way, step, h], r_recv.at[way, step, h], right if way == 0 else left)

    def row_sibling(offset, core):
        r = row.at[off(offset), core]
        return copy(r, r, rs_send.at[offset], rs_recv.at[offset], sibling)

    def z_step(s, last=False):
        slots = off(NZ - s), off(s)
        for h in range(CH):
            for way in range(2):
                r_copy(way, s - 1, h, slots[way]).wait_recv()
                if not last or h // (CH // 2) == way:
                    r_copy(way, s, h, slots[way]).start()
        row_sibling(NZ - s, k).start()
        row_sibling(s, k).start()

    def accumulate(one, two):
        def component(d, _):
            lanes = pl.ds(pl.multiple_of(d * A + k * 128, 128), 256)
            lhs = jnp.concatenate(
                [row[one, 0, :, lanes], row[one, 1, :, lanes], row[two, 0, :, lanes], row[two, 1, :, lanes]], axis=0
            )
            rhs = jnp.concatenate([col[one, 0], col[one, 1], col[two, 0], col[two, 1]], axis=0)
            acc[d] += lax.dot_general(
                lhs, rhs, (((0,), (0,)), ((), ())), preferred_element_type=jnp.float32
            )
            return 0

        lax.fori_loop(0, 3, component, 0)

    def z_compute(s):
        row_sibling(s, 1 - k).wait_recv()
        row_sibling(NZ - s, 1 - k).wait_recv()
        accumulate(off(NZ - s), off(s))

    a_copy(0, c).start()
    a_copy(1, c).start()
    have(0)
    a_copy(0, chip(3, 0)).wait_recv()
    a_copy(2, chip(3, 0)).start()
    a_copy(1, chip(1, 0)).wait_recv()
    a_copy(3, chip(1, 0)).start()

    for n in range(CH):

        @pl.when(leg_z != z)
        def _():
            leg_1(n).wait_recv()

        @pl.when(leg_p != c)
        def _():
            leg_2(n, c).start()

    @pl.when(leg_p == c)
    def _():
        row[seed, k] = mid[...]

    have(3)
    have(1)
    for n in range(CH):

        @pl.when(leg_p != c)
        def _():
            leg_2(n, seed).wait_recv()

        for way in range(2):
            r_copy(way, 0, n, seed).start()
    row_sibling(0, k).start()
    b_pass(0)
    a_copy(2, chip(2, 0)).wait_recv()
    a_copy(3, chip(2, 0)).wait_recv()
    have(2)
    b_pass(3)
    b_pass(1)
    z_step(1)
    b_pass(2)
    z_step(2)
    for oa in (0, 3, 1, 2):
        b_end(oa)

    def col_wait(q, _):
        col_sibling(q, 1 - k).wait_recv()
        return 0

    def compute(s, _):
        z_compute(s)
        return 0

    def middle(s, _):
        z_step(s)
        z_compute(s - 1)
        return 0

    z_step(3)
    lax.fori_loop(0, NZ, col_wait, 0)
    lax.fori_loop(1, 3, compute, 0)
    lax.fori_loop(4, 7, middle, 0)
    z_step(7, last=True)
    lax.fori_loop(6, 8, compute, 0)
    far = off(NZ // 2)
    for h in range(CH):
        r_copy(h // (CH // 2), NZ // 2 - 1, h, far).wait_recv()
    row_sibling(NZ // 2, k).start()
    row_sibling(0, 1 - k).wait_recv()
    row_sibling(NZ // 2, 1 - k).wait_recv()
    accumulate(seed, far)
    for i in range(3):
        for d in range(3):
            cov_ref[i, d] = acc[i, pl.ds(pl.multiple_of(k * F, F), A // 2), d * A : (d + 1) * A] * (1.0 / FRAMES)

    for p in range(2):
        over_z(lambda i, o: copy(zbuf.at[p, z], zbuf.at[p, z], z_send.at[p, i], z_recv.at[p, z], (me, o)).wait_send())
        over_p(lambda i, o: copy(pbuf.at[p, me], pbuf.at[p, me], p_send.at[p, i], p_recv.at[p, me], (o, z)).wait_send())

    for n in range(CH):

        @pl.when(leg_z != z)
        def _():
            leg_1(n).wait_send()

        @pl.when(leg_p != c)
        def _():
            leg_2(n, seed).wait_send()

    def slot_sent(q, _):
        col_sibling(q, k).wait_send()
        row_sibling(q, k).wait_send()
        return 0

    def b_sent(oa, _):
        for kind in range(4):
            b_copy(oa, kind, c).wait_send()
        return 0

    def r_sent(s, _):
        for way in range(2):
            for h in range(CH):
                r_copy(way, s, h, seed).wait_send()
        return 0

    lax.fori_loop(0, NZ, slot_sent, 0)
    for kind in range(4):
        a_copy(kind, c).wait_send()
    lax.fori_loop(0, 4, b_sent, 0)
    lax.fori_loop(0, NZ // 2 - 1, r_sent, 0)
    for h in range(CH):
        r_copy(h // (CH // 2), NZ // 2 - 1, h, seed).wait_send()


def body(frames, reference_structure):
    dma = pltpu.SemaphoreType.DMA
    vmem = pl.BlockSpec(memory_space=pltpu.VMEM)
    covariance, mean = pl.pallas_call(
        kernel,
        out_shape=(
            jax.ShapeDtypeStruct((3, 3, A // 2, A), jnp.float32),
            jax.ShapeDtypeStruct((3, A), jnp.float32),
        ),
        in_specs=[vmem, vmem],
        out_specs=(vmem, vmem),
        scratch_shapes=[
            pltpu.VMEM((4 * F, A), jnp.float32),
            pltpu.VMEM((16, A), jnp.float32),
            pltpu.VMEM((8, 4 * F), jnp.float32),
            pltpu.VMEM((16, 2 * F), jnp.float32),
            pltpu.VMEM((16, 2 * F), jnp.float32),
            pltpu.VMEM((3, F, A), jnp.float32),
            pltpu.VMEM((2, NZ, 8, 2 * F), jnp.float32),
            pltpu.VMEM((2, NP, 4, A), jnp.float32),
            pltpu.VMEM((F, W), jnp.bfloat16),
            pltpu.VMEM((NZ, 2, F, W), jnp.bfloat16),
            pltpu.VMEM((NZ, 2, F, W), jnp.bfloat16),
            pltpu.VMEM((3, 256, W), jnp.float32),
            dma((2, NZ)), dma((2, NZ)), dma((2, NP)), dma((2, NP)),
            dma((4,)), dma((4,)), dma((4, 4)), dma((4, 4)), dma((NZ,)), dma((NZ,)),
            dma((2, CH)), dma((2, CH)), dma((2, 8, CH)), dma((2, 8, CH)), dma((NZ,)), dma((NZ,)),
        ],
        compiler_params=pltpu.CompilerParams(
            collective_id=0, has_side_effects=True, vmem_limit_bytes=44 * 1024 * 1024
        ),
        cost_estimate=pl.CostEstimate(flops=3_000_000_000, bytes_accessed=8_000_000, transcendentals=0),
    )(jnp.transpose(frames, (1, 0, 2)), reference_structure)
    return jnp.transpose(covariance, (0, 2, 1, 3)), mean


def solution(mesh):
    return jax.shard_map(
        body,
        mesh=mesh,
        in_specs=(P("frames", None, "atoms"), P(None, "atoms")),
        out_specs=(P(None, "frames", None, "atoms"), P(None, "atoms")),
        check_vma=False,
    )
```

```python
import jax
import jax.numpy as jnp
from jax import lax
from jax.experimental import pallas as pl
from jax.experimental.pallas import tpu as pltpu
from jax.sharding import PartitionSpec as P

ATOMS = 6144
FRAMES = 2048
POLAR = 8
F = 64
A = 384
W = 3 * A
NZ = 16
NP = 32
H = F // 2
CH = 4
Q = F // CH
MESH = pl.DeviceIdType.MESH
HIGHEST = lax.Precision.HIGHEST


def polar_factor(cross):
    square = sum(cross[i][j] * cross[i][j] for i in range(3) for j in range(3))
    factor = jnp.sqrt(3.0 / square)
    flat = tuple(cross[i][j] * factor for i in range(3) for j in range(3))

    def turn(_, flat):
        e = [flat[0:3], flat[3:6], flat[6:9]]
        cof = [
            [
                e[(i + 1) % 3][(j + 1) % 3] * e[(i + 2) % 3][(j + 2) % 3]
                - e[(i + 1) % 3][(j + 2) % 3] * e[(i + 2) % 3][(j + 1) % 3]
                for j in range(3)
            ]
            for i in range(3)
        ]
        det = e[0][0] * cof[0][0] + e[0][1] * cof[0][1] + e[0][2] * cof[0][2]
        half = 0.5 / det
        return tuple(0.5 * e[i][j] + cof[i][j] * half for i in range(3) for j in range(3))

    flat = lax.fori_loop(0, POLAR, turn, flat)
    return [flat[0:3], flat[3:6], flat[6:9]]


def kernel(
    frames_in, ref_in, cov_ref, mean_ref,
    frames_ref, ref_ref, fa, aug, w, tile, rt, al, zbuf, pbuf, col, row, acc, in_sem,
    z_send, z_recv, p_send, p_recv,
    a_send, a_recv, b_send, b_recv, cs_send, cs_recv,
    l_send, l_recv, r_send, r_recv, rs_send, rs_recv,
):
    me = lax.axis_index("frames")
    z = lax.axis_index("atoms")
    c = me // 2
    k = me % 2
    y = c // 4
    x = c % 4
    pa = x + k * (y - x)
    pb = y + k * (x - y)
    sibling = (c * 2 + 1 - k, z)

    def copy(src, dst, send, recv, device):
        return pltpu.make_async_remote_copy(src, dst, send, recv, device_id=device, device_id_type=MESH)

    def z_other(i):
        return (z + 8 + ((i + 1) // 2) * (2 * (i % 2) - 1)) % NZ

    def p_other(i):
        return (((y + i // 8 + 2) % 4) * 4 + (x + i // 2 + 2) % 4) * 2 + (k + i) % 2

    def over_z(act):
        def turn(i, _):
            act(i, z_other(i))
            return 0

        lax.fori_loop(0, NZ - 1, turn, 0)

    def over_p(act):
        def turn(i, _):
            act(i, p_other(i))
            return 0

        lax.fori_loop(0, 20, turn, 0)
        lax.fori_loop(21, NP, turn, 0)

    get_frames = pltpu.make_async_copy(frames_in, frames_ref, in_sem.at[0])
    get_ref = pltpu.make_async_copy(ref_in, ref_ref, in_sem.at[1])
    get_frames.start()
    get_ref.start()

    leg_z = (7 * z + c + 8 * k) % NZ
    seeds = (z + 9 * c) % NZ
    seed = (seeds + 8 * k) % NZ
    moves = jnp.logical_or(z != c, leg_z != z)

    barrier = pltpu.get_barrier_semaphore()
    over_z(lambda i, o: pl.semaphore_signal(barrier, inc=1, device_id=(me, o), device_id_type=MESH))
    over_p(lambda i, o: pl.semaphore_signal(barrier, inc=1, device_id=(o, z), device_id_type=MESH))

    @pl.when(moves)
    def _():
        pl.semaphore_signal(barrier, inc=1, device_id=(seed * 2 + k, c), device_id_type=MESH)

    get_frames.wait()
    get_ref.wait()
    fa[0:F, :] = frames_ref[0]
    fa[F : 2 * F, :] = frames_ref[2]
    fa[2 * F : 3 * F, :] = frames_ref[1]
    fa[3 * F : 4 * F, :] = jnp.ones((F, A), jnp.float32)
    aug[...] = jnp.zeros((16, A), jnp.float32)
    aug[3:4, :] = jnp.ones((1, A), jnp.float32)
    aug[15:16, :] = jnp.ones((1, A), jnp.float32)
    w[...] = jnp.zeros((8, 4 * F), jnp.float32)
    rt[...] = jnp.zeros((16, 2 * F), jnp.float32)
    acc[...] = jnp.zeros((3, 256, W), jnp.float32)
    low = lax.broadcasted_iota(jnp.int32, (1, 2 * F), 1) < F

    def local_sums():
        nt = (((1,), (1,)), ((), ()))
        first = lax.dot_general(
            aug[0:8, :], fa[0 : 2 * F, :], nt, precision=HIGHEST, preferred_element_type=jnp.float32
        )
        second = lax.dot_general(
            aug[8:16, :], fa[2 * F : 4 * F, :], nt, precision=HIGHEST, preferred_element_type=jnp.float32
        )
        return first + second

    mean_now = ref_ref[...]
    for p in range(2):
        aug[0:3, :] = mean_now
        aug[12:15, :] = mean_now
        zbuf[p, z] = local_sums()
        if p == 0:
            pl.semaphore_wait(barrier, NZ + NP - 2 + jnp.where(moves, 1, 0))

        def z_copy(i, o, slot):
            return copy(zbuf.at[p, slot], zbuf.at[p, slot], z_send.at[p, i], z_recv.at[p, slot], (me, o))

        over_z(lambda i, o: z_copy(i, o, z).start())
        over_z(lambda i, o: z_copy(i, o, o).wait_recv())
        total = zbuf[p, 0]
        for i in range(1, NZ):
            total = total + zbuf[p, i]
        tile[0:8, :] = total
        tile[8:16, :] = pltpu.roll(total, F, 1)
        centroid = [tile[r : r + 1, :] / ATOMS for r in (3, 7, 11)]
        cross = [
            [tile[4 * i + d : 4 * i + d + 1, :] - centroid[i] * tile[12 + d : 13 + d, :] for d in range(3)]
            for i in range(3)
        ]
        rotation = polar_factor(cross)
        for d in range(3):
            back = -(
                rotation[0][d] * centroid[0] + rotation[1][d] * centroid[1] + rotation[2][d] * centroid[2]
            )
            w[d : d + 1, 0 : 2 * F] = jnp.where(low, rotation[0][d], pltpu.roll(rotation[2][d], F, 1))
            w[d : d + 1, 2 * F : 4 * F] = jnp.where(low, rotation[1][d], pltpu.roll(back, F, 1))
        part = lax.dot_general(
            w[...], fa[...], (((1,), (0,)), ((), ())), precision=HIGHEST, preferred_element_type=jnp.float32
        )
        pbuf[p, me] = part[0:4, :]

        def p_copy(i, o, slot):
            return copy(pbuf.at[p, slot], pbuf.at[p, slot], p_send.at[p, i], p_recv.at[p, slot], (o, z))

        over_p(lambda i, o: p_copy(i, o, me).start())
        if p == 1:
            for i in range(3):
                for d in range(3):
                    rt[3 * i + d : 3 * i + d + 1, :] = rotation[i][d]
                rt[9 + i : 10 + i, :] = centroid[i]
            columns = jnp.transpose(rt[...])[0:F, :]
            shifted = [frames_ref[i] - columns[:, 9 + i : 10 + i] for i in range(3)]
            for d in range(3):
                al[d] = sum(columns[:, 3 * i + d : 3 * i + d + 1] * shifted[i] for i in range(3))
        over_p(lambda i, o: p_copy(i, o, o).wait_recv())
        summed = pbuf[p, 0]
        for i in range(1, NP):
            summed = summed + pbuf[p, i]
        mean_now = summed[0:3, :] / FRAMES

    mean_ref[...] = mean_now
    for d in range(3):
        col[c, k, :, d * A : (d + 1) * A] = (al[d] - mean_now[d : d + 1, :]).astype(jnp.bfloat16)

    def leg(n, slot):
        rows = pl.ds(n * Q, Q)
        return copy(
            col.at[c, k, rows], row.at[slot, k, rows], l_send.at[n], l_recv.at[n], (z * 2 + k, leg_z)
        )

    @pl.when(moves)
    def _():
        for n in range(CH):
            leg(n, c).start()

    @pl.when(jnp.logical_not(moves))
    def _():
        row[seed, k] = col[c, k]

    def chip(oa, ob):
        qa, qb = (pa + oa) % 4, (pb + ob) % 4
        return (qb + k * (qa - qb)) * 4 + qa + k * (qb - qa)

    def at(oa, ob):
        return (chip(oa, ob) * 2 + k, z)

    def part_of(slot, half):
        if half is None:
            return col.at[slot, k]
        return col.at[slot, k, half * H : (half + 1) * H]

    HALF = (None, None, 0, 1)
    TOWARD = (1, 3, 1, 3)

    def a_copy(kind, slot):
        r = part_of(slot, HALF[kind])
        return copy(r, r, a_send.at[kind], a_recv.at[kind], at(TOWARD[kind], 0))

    def b_copy(oa, kind, slot):
        r = part_of(slot, HALF[kind])
        return copy(r, r, b_send.at[oa, kind], b_recv.at[oa, kind], at(0, TOWARD[kind]))

    def col_sibling(slot, core):
        r = col.at[slot, core]
        return copy(r, r, cs_send.at[slot], cs_recv.at[slot], sibling)

    def have(oa):
        slot = chip(oa, 0)
        b_copy(oa, 0, slot).start()
        b_copy(oa, 1, slot).start()
        col_sibling(slot, k).start()

    def b_pass(oa):
        before, after = chip(oa, 3), chip(oa, 1)
        b_copy(oa, 0, before).wait_recv()
        b_copy(oa, 2, before).start()
        col_sibling(before, k).start()
        b_copy(oa, 1, after).wait_recv()
        b_copy(oa, 3, after).start()
        col_sibling(after, k).start()

    def b_end(oa):
        slot = chip(oa, 2)
        b_copy(oa, 2, slot).wait_recv()
        b_copy(oa, 3, slot).wait_recv()
        col_sibling(slot, k).start()

    right, left = (me, (z + 1) % NZ), (me, (z + NZ - 1) % NZ)

    def off(offset):
        return (seed + offset) % NZ

    def r_copy(way, step, h, slot):
        r = row.at[slot, k, h * Q : (h + 1) * Q]
        return copy(r, r, r_send.at[way, step, h], r_recv.at[way, step, h], right if way == 0 else left)

    def row_sibling(offset, core):
        r = row.at[(seeds + 8 * core + offset) % NZ, core]
        return copy(r, r, rs_send.at[offset], rs_recv.at[offset], sibling)

    def z_step(s, last=False):
        slots = off(NZ - s), off(s)
        for h in range(CH):
            for way in range(2):
                r_copy(way, s - 1, h, slots[way]).wait_recv()
                if not last or h // (CH // 2) == way:
                    r_copy(way, s, h, slots[way]).start()
        row_sibling(NZ - s, k).start()
        row_sibling(s, k).start()

    def accumulate(one, two, last=False):
        pieces = [((seeds + 8 * core + o) % NZ, core) for o in (one, two) for core in range(2)]

        def component(i, _):
            lanes = pl.ds(pl.multiple_of(i * A + k * 128, 128), 256)
            lhs = jnp.concatenate([row[q, core, :, lanes] for q, core in pieces], axis=0)
            rhs = jnp.concatenate([col[q, core] for q, core in pieces], axis=0)
            total = acc[i] + lax.dot_general(
                lhs, rhs, (((0,), (0,)), ((), ())), preferred_element_type=jnp.float32
            )
            if not last:
                acc[i] = total
                return 0
            kept = jnp.where(k == 0, total[0 : A // 2], total[F : F + A // 2]) * (1.0 / FRAMES)
            for d in range(3):
                cov_ref[i, d] = kept[:, d * A : (d + 1) * A]
            return 0

        lax.fori_loop(0, 3, component, 0)

    def z_compute(s):
        row_sibling(s, 1 - k).wait_recv()
        row_sibling(NZ - s, 1 - k).wait_recv()
        accumulate(NZ - s, s)

    a_copy(0, c).start()
    a_copy(1, c).start()
    have(0)
    a_copy(0, chip(3, 0)).wait_recv()
    a_copy(2, chip(3, 0)).start()
    a_copy(1, chip(1, 0)).wait_recv()
    a_copy(3, chip(1, 0)).start()

    have(3)
    have(1)
    for n in range(CH):

        @pl.when(moves)
        def _():
            leg(n, seed).wait_recv()

        for way in range(2):
            r_copy(way, 0, n, seed).start()
    row_sibling(0, k).start()
    b_pass(0)
    a_copy(2, chip(2, 0)).wait_recv()
    a_copy(3, chip(2, 0)).wait_recv()
    have(2)
    b_pass(3)
    b_pass(1)
    z_step(1)
    b_pass(2)
    z_step(2)
    for oa in (0, 3, 1, 2):
        b_end(oa)

    def col_wait(q, _):
        col_sibling(q, 1 - k).wait_recv()
        return 0

    def compute(s, _):
        z_compute(s)
        return 0

    def middle(s, _):
        z_step(s)
        z_compute(s - 1)
        return 0

    z_step(3)
    lax.fori_loop(0, NZ, col_wait, 0)
    lax.fori_loop(1, 3, compute, 0)
    lax.fori_loop(4, 7, middle, 0)
    z_step(7, last=True)
    lax.fori_loop(6, 8, compute, 0)
    far = off(NZ // 2)
    for h in range(CH):
        r_copy(h // (CH // 2), NZ // 2 - 1, h, far).wait_recv()
    row_sibling(NZ // 2, k).start()
    row_sibling(0, 1 - k).wait_recv()
    row_sibling(NZ // 2, 1 - k).wait_recv()
    accumulate(0, NZ // 2, last=True)

    for p in range(2):
        over_z(lambda i, o: copy(zbuf.at[p, z], zbuf.at[p, z], z_send.at[p, i], z_recv.at[p, z], (me, o)).wait_send())
        over_p(lambda i, o: copy(pbuf.at[p, me], pbuf.at[p, me], p_send.at[p, i], p_recv.at[p, me], (o, z)).wait_send())

    for n in range(CH):

        @pl.when(moves)
        def _():
            leg(n, seed).wait_send()

    def slot_sent(q, _):
        col_sibling(q, k).wait_send()
        row_sibling(q, k).wait_send()
        return 0

    def b_sent(oa, _):
        for kind in range(4):
            b_copy(oa, kind, c).wait_send()
        return 0

    def r_sent(s, _):
        for way in range(2):
            for h in range(CH):
                r_copy(way, s, h, seed).wait_send()
        return 0

    lax.fori_loop(0, NZ, slot_sent, 0)
    for kind in range(4):
        a_copy(kind, c).wait_send()
    lax.fori_loop(0, 4, b_sent, 0)
    lax.fori_loop(0, NZ // 2 - 1, r_sent, 0)
    for h in range(CH):
        r_copy(h // (CH // 2), NZ // 2 - 1, h, seed).wait_send()


def body(frames, reference_structure):
    dma = pltpu.SemaphoreType.DMA
    vmem = pl.BlockSpec(memory_space=pltpu.VMEM)
    hbm = pl.BlockSpec(memory_space=pltpu.HBM)
    covariance, mean = pl.pallas_call(
        kernel,
        out_shape=(
            jax.ShapeDtypeStruct((3, 3, A // 2, A), jnp.float32),
            jax.ShapeDtypeStruct((3, A), jnp.float32),
        ),
        in_specs=[hbm, hbm],
        out_specs=(vmem, vmem),
        scratch_shapes=[
            pltpu.VMEM((3, F, A), jnp.float32),
            pltpu.VMEM((3, A), jnp.float32),
            pltpu.VMEM((4 * F, A), jnp.float32),
            pltpu.VMEM((16, A), jnp.float32),
            pltpu.VMEM((8, 4 * F), jnp.float32),
            pltpu.VMEM((16, 2 * F), jnp.float32),
            pltpu.VMEM((16, 2 * F), jnp.float32),
            pltpu.VMEM((3, F, A), jnp.float32),
            pltpu.VMEM((2, NZ, 8, 2 * F), jnp.float32),
            pltpu.VMEM((2, NP, 4, A), jnp.float32),
            pltpu.VMEM((NZ, 2, F, W), jnp.bfloat16),
            pltpu.VMEM((NZ, 2, F, W), jnp.bfloat16),
            pltpu.VMEM((3, 256, W), jnp.float32),
            dma((2,)),
            dma((2, NZ)), dma((2, NZ)), dma((2, NP)), dma((2, NP)),
            dma((4,)), dma((4,)), dma((4, 4)), dma((4, 4)), dma((NZ,)), dma((NZ,)),
            dma((CH,)), dma((CH,)), dma((2, 8, CH)), dma((2, 8, CH)), dma((NZ,)), dma((NZ,)),
        ],
        compiler_params=pltpu.CompilerParams(
            collective_id=0, has_side_effects=True, vmem_limit_bytes=44 * 1024 * 1024
        ),
        cost_estimate=pl.CostEstimate(flops=3_000_000_000, bytes_accessed=8_000_000, transcendentals=0),
    )(jnp.transpose(frames, (1, 0, 2)), reference_structure)
    return jnp.transpose(covariance, (0, 2, 1, 3)), mean


def solution(mesh):
    return jax.shard_map(
        body,
        mesh=mesh,
        in_specs=(P("frames", None, "atoms"), P(None, "atoms")),
        out_specs=(P(None, "frames", None, "atoms"), P(None, "atoms")),
        check_vma=False,
    )
```

```python
import jax
import jax.numpy as jnp
from jax import lax
from jax.experimental import pallas as pl
from jax.experimental.pallas import tpu as pltpu
from jax.sharding import PartitionSpec as P

ATOMS = 6144
FRAMES = 2048
POLAR = 8
F = 64
A = 384
W = 3 * A
NZ = 16
NP = 32
H = F // 2
CH = 4
Q = F // CH
MESH = pl.DeviceIdType.MESH
HIGHEST = lax.Precision.HIGHEST


def polar_factor(cross):
    square = sum(cross[i][j] * cross[i][j] for i in range(3) for j in range(3))
    factor = jnp.sqrt(3.0 / square)
    flat = tuple(cross[i][j] * factor for i in range(3) for j in range(3))

    def turn(_, flat):
        e = [flat[0:3], flat[3:6], flat[6:9]]
        cof = [
            [
                e[(i + 1) % 3][(j + 1) % 3] * e[(i + 2) % 3][(j + 2) % 3]
                - e[(i + 1) % 3][(j + 2) % 3] * e[(i + 2) % 3][(j + 1) % 3]
                for j in range(3)
            ]
            for i in range(3)
        ]
        det = e[0][0] * cof[0][0] + e[0][1] * cof[0][1] + e[0][2] * cof[0][2]
        half = 0.5 / det
        return tuple(0.5 * e[i][j] + cof[i][j] * half for i in range(3) for j in range(3))

    flat = lax.fori_loop(0, POLAR, turn, flat)
    return [flat[0:3], flat[3:6], flat[6:9]]


def kernel(
    frames_in, ref_in, cov_ref, mean_ref,
    frames_ref, ref_ref, fa, aug, w, tile, rt, al, zbuf, pbuf, col, row, acc, in_sem,
    z_send, z_recv, p_send, p_recv,
    a_send, a_recv, b_send, b_recv, cs_send, cs_recv,
    l_send, l_recv, r_send, r_recv, rs_send, rs_recv,
):
    me = lax.axis_index("frames")
    z = lax.axis_index("atoms")
    c = me // 2
    k = me % 2
    y = c // 4
    x = c % 4
    pa = x + k * (y - x)
    pb = y + k * (x - y)
    sibling = (c * 2 + 1 - k, z)

    def copy(src, dst, send, recv, device):
        return pltpu.make_async_remote_copy(src, dst, send, recv, device_id=device, device_id_type=MESH)

    def all_of(sized, semaphore):
        pltpu.make_async_copy(sized, sized, semaphore).wait()

    def z_other(i):
        return (z + 8 + ((i + 1) // 2) * (2 * (i % 2) - 1)) % NZ

    def p_other(i):
        return (((y + i // 8 + 2) % 4) * 4 + (x + i // 2 + 2) % 4) * 2 + (k + i) % 2

    def over_z(act):
        def turn(i, _):
            act(i, z_other(i))
            return 0

        lax.fori_loop(0, NZ - 1, turn, 0)

    def over_p(act):
        def turn(i, _):
            act(i, p_other(i))
            return 0

        lax.fori_loop(0, 20, turn, 0)
        lax.fori_loop(21, NP, turn, 0)

    get_frames = pltpu.make_async_copy(frames_in, frames_ref, in_sem.at[0])
    get_ref = pltpu.make_async_copy(ref_in, ref_ref, in_sem.at[1])
    get_frames.start()
    get_ref.start()

    leg_z = (7 * z + c + 8 * k) % NZ
    seeds = (z + 9 * c) % NZ
    seed = (seeds + 8 * k) % NZ
    moves = jnp.logical_or(z != c, leg_z != z)

    barrier = pltpu.get_barrier_semaphore()
    over_z(lambda i, o: pl.semaphore_signal(barrier, inc=1, device_id=(me, o), device_id_type=MESH))
    over_p(lambda i, o: pl.semaphore_signal(barrier, inc=1, device_id=(o, z), device_id_type=MESH))

    @pl.when(moves)
    def _():
        pl.semaphore_signal(barrier, inc=1, device_id=(seed * 2 + k, c), device_id_type=MESH)

    get_frames.wait()
    get_ref.wait()
    fa[0:F, :] = frames_ref[0]
    fa[F : 2 * F, :] = frames_ref[2]
    fa[2 * F : 3 * F, :] = frames_ref[1]
    fa[3 * F : 4 * F, :] = jnp.ones((F, A), jnp.float32)
    aug[...] = jnp.zeros((16, A), jnp.float32)
    aug[3:4, :] = jnp.ones((1, A), jnp.float32)
    aug[15:16, :] = jnp.ones((1, A), jnp.float32)
    w[...] = jnp.zeros((8, 4 * F), jnp.float32)
    rt[...] = jnp.zeros((16, 2 * F), jnp.float32)
    acc[...] = jnp.zeros((3, 256, W), jnp.float32)
    low = lax.broadcasted_iota(jnp.int32, (1, 2 * F), 1) < F

    def local_sums():
        nt = (((1,), (1,)), ((), ()))
        first = lax.dot_general(
            aug[0:8, :], fa[0 : 2 * F, :], nt, precision=HIGHEST, preferred_element_type=jnp.float32
        )
        second = lax.dot_general(
            aug[8:16, :], fa[2 * F : 4 * F, :], nt, precision=HIGHEST, preferred_element_type=jnp.float32
        )
        return first + second

    mean_now = ref_ref[...]
    for p in range(2):
        aug[0:3, :] = mean_now
        aug[12:15, :] = mean_now
        zbuf[p, z] = local_sums()
        if p == 0:
            pl.semaphore_wait(barrier, NZ + NP - 2 + jnp.where(moves, 1, 0))

        def z_copy(o, slot):
            return copy(zbuf.at[p, slot], zbuf.at[p, slot], z_send.at[p], z_recv.at[p], (me, o))

        over_z(lambda i, o: z_copy(o, z).start())
        all_of(zbuf.at[p, 0 : NZ - 1], z_recv.at[p])
        total = zbuf[p, 0]
        for i in range(1, NZ):
            total = total + zbuf[p, i]
        tile[0:8, :] = total
        tile[8:16, :] = pltpu.roll(total, F, 1)
        centroid = [tile[r : r + 1, :] / ATOMS for r in (3, 7, 11)]
        cross = [
            [tile[4 * i + d : 4 * i + d + 1, :] - centroid[i] * tile[12 + d : 13 + d, :] for d in range(3)]
            for i in range(3)
        ]
        rotation = polar_factor(cross)
        for d in range(3):
            back = -(
                rotation[0][d] * centroid[0] + rotation[1][d] * centroid[1] + rotation[2][d] * centroid[2]
            )
            w[d : d + 1, 0 : 2 * F] = jnp.where(low, rotation[0][d], pltpu.roll(rotation[2][d], F, 1))
            w[d : d + 1, 2 * F : 4 * F] = jnp.where(low, rotation[1][d], pltpu.roll(back, F, 1))
        part = lax.dot_general(
            w[...], fa[...], (((1,), (0,)), ((), ())), precision=HIGHEST, preferred_element_type=jnp.float32
        )
        pbuf[p, me] = part[0:4, :]

        def p_copy(o, slot):
            return copy(pbuf.at[p, slot], pbuf.at[p, slot], p_send.at[p], p_recv.at[p], (o, z))

        over_p(lambda i, o: p_copy(o, me).start())
        if p == 1:
            for i in range(3):
                for d in range(3):
                    rt[3 * i + d : 3 * i + d + 1, :] = rotation[i][d]
                rt[9 + i : 10 + i, :] = centroid[i]
            columns = jnp.transpose(rt[...])[0:F, :]
            shifted = [frames_ref[i] - columns[:, 9 + i : 10 + i] for i in range(3)]
            for d in range(3):
                al[d] = sum(columns[:, 3 * i + d : 3 * i + d + 1] * shifted[i] for i in range(3))
        all_of(pbuf.at[p, 0 : NP - 1], p_recv.at[p])
        summed = pbuf[p, 0]
        for i in range(1, NP):
            summed = summed + pbuf[p, i]
        mean_now = summed[0:3, :] / FRAMES

    mean_ref[...] = mean_now
    for d in range(3):
        col[me, :, d * A : (d + 1) * A] = (al[d] - mean_now[d : d + 1, :]).astype(jnp.bfloat16)

    def leg(n, slot):
        rows = pl.ds(n * Q, Q)
        return copy(
            col.at[me, rows], row.at[slot * 2 + k, rows], l_send, l_recv.at[n], (z * 2 + k, leg_z)
        )

    @pl.when(moves)
    def _():
        for n in range(CH):
            leg(n, c).start()

    @pl.when(jnp.logical_not(moves))
    def _():
        row[seed * 2 + k] = col[me]

    def chip(oa, ob):
        qa, qb = (pa + oa) % 4, (pb + ob) % 4
        return (qb + k * (qa - qb)) * 4 + qa + k * (qb - qa)

    def at(oa, ob):
        return (chip(oa, ob) * 2 + k, z)

    def part_of(slot, half):
        if half is None:
            return col.at[slot * 2 + k]
        return col.at[slot * 2 + k, half * H : (half + 1) * H]

    HALF = (None, None, 0, 1)
    TOWARD = (1, 3, 1, 3)

    def a_copy(kind, slot):
        r = part_of(slot, HALF[kind])
        return copy(r, r, a_send, a_recv.at[kind], at(TOWARD[kind], 0))

    def b_copy(oa, kind, slot):
        r = part_of(slot, HALF[kind])
        return copy(r, r, b_send, b_recv.at[oa, kind], at(0, TOWARD[kind]))

    def col_sibling(slot, core):
        r = col.at[slot * 2 + core]
        return copy(r, r, cs_send, cs_recv, sibling)

    def have(oa):
        slot = chip(oa, 0)
        b_copy(oa, 0, slot).start()
        b_copy(oa, 1, slot).start()
        col_sibling(slot, k).start()

    def b_pass(oa):
        before, after = chip(oa, 3), chip(oa, 1)
        b_copy(oa, 0, before).wait_recv()
        b_copy(oa, 2, before).start()
        col_sibling(before, k).start()
        b_copy(oa, 1, after).wait_recv()
        b_copy(oa, 3, after).start()
        col_sibling(after, k).start()

    def b_end(oa):
        slot = chip(oa, 2)
        b_copy(oa, 2, slot).wait_recv()
        b_copy(oa, 3, slot).wait_recv()
        col_sibling(slot, k).start()

    right, left = (me, (z + 1) % NZ), (me, (z + NZ - 1) % NZ)

    def off(offset):
        return (seed + offset) % NZ

    def r_copy(way, step, h, slot):
        r = row.at[slot * 2 + k, h * Q : (h + 1) * Q]
        return copy(r, r, r_send, r_recv.at[way, step, h], right if way == 0 else left)

    def row_sibling(offset, core):
        r = row.at[(seeds + 8 * core + offset) % NZ * 2 + core]
        return copy(r, r, rs_send, rs_recv.at[offset], sibling)

    def z_step(s, last=False):
        slots = off(NZ - s), off(s)
        for h in range(CH):
            for way in range(2):
                r_copy(way, s - 1, h, slots[way]).wait_recv()
                if not last or h // (CH // 2) == way:
                    r_copy(way, s, h, slots[way]).start()
        row_sibling(NZ - s, k).start()
        row_sibling(s, k).start()

    def accumulate(one, two, last=False):
        pieces = [(seeds + 8 * core + o) % NZ * 2 + core for o in (one, two) for core in range(2)]

        def component(i, _):
            lanes = pl.ds(pl.multiple_of(i * A + k * 128, 128), 256)
            lhs = jnp.concatenate([row[q, :, lanes] for q in pieces], axis=0)
            rhs = jnp.concatenate([col[q] for q in pieces], axis=0)
            total = acc[i] + lax.dot_general(
                lhs, rhs, (((0,), (0,)), ((), ())), preferred_element_type=jnp.float32
            )
            if not last:
                acc[i] = total
                return 0
            kept = jnp.where(k == 0, total[0 : A // 2], total[F : F + A // 2]) * (1.0 / FRAMES)
            for d in range(3):
                cov_ref[i, d] = kept[:, d * A : (d + 1) * A]
            return 0

        lax.fori_loop(0, 3, component, 0)

    def z_compute(s):
        row_sibling(s, 1 - k).wait_recv()
        row_sibling(NZ - s, 1 - k).wait_recv()
        accumulate(NZ - s, s)

    a_copy(0, c).start()
    a_copy(1, c).start()
    have(0)
    a_copy(0, chip(3, 0)).wait_recv()
    a_copy(2, chip(3, 0)).start()
    a_copy(1, chip(1, 0)).wait_recv()
    a_copy(3, chip(1, 0)).start()

    have(3)
    have(1)
    for n in range(CH):

        @pl.when(moves)
        def _():
            leg(n, seed).wait_recv()

        for way in range(2):
            r_copy(way, 0, n, seed).start()
    row_sibling(0, k).start()
    b_pass(0)
    a_copy(2, chip(2, 0)).wait_recv()
    a_copy(3, chip(2, 0)).wait_recv()
    have(2)
    b_pass(3)
    b_pass(1)
    z_step(1)
    b_pass(2)
    z_step(2)
    for oa in (0, 3, 1, 2):
        b_end(oa)

    def compute(s, _):
        z_compute(s)
        return 0

    def middle(s, _):
        z_step(s)
        z_compute(s - 1)
        return 0

    z_step(3)
    all_of(col.at[0:NZ], cs_recv)
    lax.fori_loop(1, 3, compute, 0)
    lax.fori_loop(4, 7, middle, 0)
    z_step(7, last=True)
    lax.fori_loop(6, 8, compute, 0)
    far = off(NZ // 2)
    for p in range(2):
        all_of(zbuf.at[p, 0 : NZ - 1], z_send.at[p])
        all_of(pbuf.at[p, 0 : NP - 1], p_send.at[p])

    @pl.when(moves)
    def _():
        all_of(col.at[0], l_send)

    all_of(col.at[0:3], a_send)
    all_of(col.at[0:12], b_send)
    all_of(col.at[0:NZ], cs_send)
    for h in range(CH):
        r_copy(h // (CH // 2), NZ // 2 - 1, h, far).wait_recv()
    row_sibling(NZ // 2, k).start()
    row_sibling(0, 1 - k).wait_recv()
    row_sibling(NZ // 2, 1 - k).wait_recv()
    accumulate(0, NZ // 2, last=True)
    all_of(row.at[0 : NZ - 1], r_send)
    all_of(row.at[0:NZ], rs_send)


def body(frames, reference_structure):
    dma = pltpu.SemaphoreType.DMA
    vmem = pl.BlockSpec(memory_space=pltpu.VMEM)
    hbm = pl.BlockSpec(memory_space=pltpu.HBM)
    covariance, mean = pl.pallas_call(
        kernel,
        out_shape=(
            jax.ShapeDtypeStruct((3, 3, A // 2, A), jnp.float32),
            jax.ShapeDtypeStruct((3, A), jnp.float32),
        ),
        in_specs=[hbm, hbm],
        out_specs=(vmem, vmem),
        scratch_shapes=[
            pltpu.VMEM((3, F, A), jnp.float32),
            pltpu.VMEM((3, A), jnp.float32),
            pltpu.VMEM((4 * F, A), jnp.float32),
            pltpu.VMEM((16, A), jnp.float32),
            pltpu.VMEM((8, 4 * F), jnp.float32),
            pltpu.VMEM((16, 2 * F), jnp.float32),
            pltpu.VMEM((16, 2 * F), jnp.float32),
            pltpu.VMEM((3, F, A), jnp.float32),
            pltpu.VMEM((2, NZ, 8, 2 * F), jnp.float32),
            pltpu.VMEM((2, NP, 4, A), jnp.float32),
            pltpu.VMEM((NP, F, W), jnp.bfloat16),
            pltpu.VMEM((NP, F, W), jnp.bfloat16),
            pltpu.VMEM((3, 256, W), jnp.float32),
            dma((2,)),
            dma((2,)), dma((2,)), dma((2,)), dma((2,)),
            dma, dma((4,)), dma, dma((4, 4)), dma, dma,
            dma, dma((CH,)), dma, dma((2, 8, CH)), dma, dma((NZ,)),
        ],
        compiler_params=pltpu.CompilerParams(
            collective_id=0, has_side_effects=True, vmem_limit_bytes=44 * 1024 * 1024
        ),
        cost_estimate=pl.CostEstimate(flops=3_000_000_000, bytes_accessed=8_000_000, transcendentals=0),
    )(jnp.transpose(frames, (1, 0, 2)), reference_structure)
    return jnp.transpose(covariance, (0, 2, 1, 3)), mean


def solution(mesh):
    return jax.shard_map(
        body,
        mesh=mesh,
        in_specs=(P("frames", None, "atoms"), P(None, "atoms")),
        out_specs=(P(None, "frames", None, "atoms"), P(None, "atoms")),
        check_vma=False,
    )
```

```python
import jax
import jax.numpy as jnp
from jax import lax
from jax.experimental import pallas as pl
from jax.experimental.pallas import tpu as pltpu
from jax.sharding import PartitionSpec as P

ATOMS = 6144
FRAMES = 2048
POLAR = 8
F = 64
A = 384
W = 3 * A
NZ = 16
NP = 32
H = F // 2
CH = 4
Q = F // CH
MESH = pl.DeviceIdType.MESH
HIGHEST = lax.Precision.HIGHEST


def polar_factor(cross):
    square = sum(cross[i][j] * cross[i][j] for i in range(3) for j in range(3))
    factor = jnp.sqrt(3.0 / square)
    flat = tuple(cross[i][j] * factor for i in range(3) for j in range(3))

    def turn(_, flat):
        e = [flat[0:3], flat[3:6], flat[6:9]]
        cof = [
            [
                e[(i + 1) % 3][(j + 1) % 3] * e[(i + 2) % 3][(j + 2) % 3]
                - e[(i + 1) % 3][(j + 2) % 3] * e[(i + 2) % 3][(j + 1) % 3]
                for j in range(3)
            ]
            for i in range(3)
        ]
        det = e[0][0] * cof[0][0] + e[0][1] * cof[0][1] + e[0][2] * cof[0][2]
        half = 0.5 / det
        return tuple(0.5 * e[i][j] + cof[i][j] * half for i in range(3) for j in range(3))

    flat = lax.fori_loop(0, POLAR, turn, flat)
    return [flat[0:3], flat[3:6], flat[6:9]]


def kernel(
    frames_in, ref_in, cov_ref, mean_ref,
    frames_ref, ref_ref, fa, aug, w, tile, rt, al, zbuf, pbuf, col, row, acc, in_sem,
    z_send, z_recv, p_send, p_recv,
    a_send, a_recv, b_send, b_recv, cs_send, cs_recv,
    l_send, l_recv, r_send, r_recv, rs_send, rs_recv,
):
    me = lax.axis_index("frames")
    z = lax.axis_index("atoms")
    c = me // 2
    k = me % 2
    y = c // 4
    x = c % 4
    pa = x + k * (y - x)
    pb = y + k * (x - y)
    sibling = (c * 2 + 1 - k, z)

    def copy(src, dst, send, recv, device):
        return pltpu.make_async_remote_copy(src, dst, send, recv, device_id=device, device_id_type=MESH)

    def all_of(sized, semaphore):
        pltpu.make_async_copy(sized, sized, semaphore).wait()

    def z_other(i):
        return (z + 8 + ((i + 1) // 2) * (2 * (i % 2) - 1)) % NZ

    def p_other(i):
        return (((y + i // 8 + 2) % 4) * 4 + (x + i // 2 + 2) % 4) * 2 + (k + i) % 2

    def over_z(act):
        def turn(i, _):
            act(i, z_other(i))
            return 0

        lax.fori_loop(0, NZ - 1, turn, 0)

    def over_p(act):
        def turn(i, _):
            act(i, p_other(i))
            return 0

        lax.fori_loop(0, 20, turn, 0)
        lax.fori_loop(21, NP, turn, 0)

    get_frames = pltpu.make_async_copy(frames_in, frames_ref, in_sem.at[0])
    get_ref = pltpu.make_async_copy(ref_in, ref_ref, in_sem.at[1])
    get_frames.start()
    get_ref.start()

    leg_z = (7 * z + c + 8 * k) % NZ
    seeds = (z + 9 * c) % NZ
    seed = (seeds + 8 * k) % NZ
    moves = jnp.logical_or(z != c, leg_z != z)

    barrier = pltpu.get_barrier_semaphore()

    @pl.when(moves)
    def _():
        pl.semaphore_signal(barrier, inc=1, device_id=(seed * 2 + k, c), device_id_type=MESH)

    over_z(lambda i, o: pl.semaphore_signal(barrier, inc=1, device_id=(me, o), device_id_type=MESH))
    over_p(lambda i, o: pl.semaphore_signal(barrier, inc=1, device_id=(o, z), device_id_type=MESH))

    get_frames.wait()
    get_ref.wait()
    fa[0:F, :] = frames_ref[0]
    fa[F : 2 * F, :] = frames_ref[2]
    fa[2 * F : 3 * F, :] = frames_ref[1]
    fa[3 * F : 4 * F, :] = jnp.ones((F, A), jnp.float32)
    aug[...] = jnp.zeros((16, A), jnp.float32)
    aug[3:4, :] = jnp.ones((1, A), jnp.float32)
    aug[15:16, :] = jnp.ones((1, A), jnp.float32)
    w[...] = jnp.zeros((8, 4 * F), jnp.float32)
    rt[...] = jnp.zeros((16, 2 * F), jnp.float32)
    acc[...] = jnp.zeros((3, 256, W), jnp.float32)
    low = lax.broadcasted_iota(jnp.int32, (1, 2 * F), 1) < F

    def local_sums():
        nt = (((1,), (1,)), ((), ()))
        first = lax.dot_general(
            aug[0:8, :], fa[0 : 2 * F, :], nt, precision=HIGHEST, preferred_element_type=jnp.float32
        )
        second = lax.dot_general(
            aug[8:16, :], fa[2 * F : 4 * F, :], nt, precision=HIGHEST, preferred_element_type=jnp.float32
        )
        return first + second

    mean_now = ref_ref[...]
    for p in range(2):
        aug[0:3, :] = mean_now
        aug[12:15, :] = mean_now
        zbuf[p, z] = local_sums()
        if p == 0:
            pl.semaphore_wait(barrier, NZ + NP - 2 + jnp.where(moves, 1, 0))

        def z_copy(o, slot):
            return copy(zbuf.at[p, slot], zbuf.at[p, slot], z_send.at[p], z_recv.at[p], (me, o))

        over_z(lambda i, o: z_copy(o, z).start())
        all_of(zbuf.at[p, 0 : NZ - 1], z_recv.at[p])
        total = zbuf[p, 0]
        for i in range(1, NZ):
            total = total + zbuf[p, i]
        tile[0:8, :] = total
        tile[8:16, :] = pltpu.roll(total, F, 1)
        centroid = [tile[r : r + 1, :] / ATOMS for r in (3, 7, 11)]
        cross = [
            [tile[4 * i + d : 4 * i + d + 1, :] - centroid[i] * tile[12 + d : 13 + d, :] for d in range(3)]
            for i in range(3)
        ]
        rotation = polar_factor(cross)
        for d in range(3):
            back = -(
                rotation[0][d] * centroid[0] + rotation[1][d] * centroid[1] + rotation[2][d] * centroid[2]
            )
            w[d : d + 1, 0 : 2 * F] = jnp.where(low, rotation[0][d], pltpu.roll(rotation[2][d], F, 1))
            w[d : d + 1, 2 * F : 4 * F] = jnp.where(low, rotation[1][d], pltpu.roll(back, F, 1))
        part = lax.dot_general(
            w[...], fa[...], (((1,), (0,)), ((), ())), precision=HIGHEST, preferred_element_type=jnp.float32
        )
        pbuf[p, me] = part[0:4, :]

        def p_copy(o, slot):
            return copy(pbuf.at[p, slot], pbuf.at[p, slot], p_send.at[p], p_recv.at[p], (o, z))

        over_p(lambda i, o: p_copy(o, me).start())
        if p == 1:
            for i in range(3):
                for d in range(3):
                    rt[3 * i + d : 3 * i + d + 1, :] = rotation[i][d]
                rt[9 + i : 10 + i, :] = centroid[i]
            columns = jnp.transpose(rt[...])[0:F, :]
            shifted = [frames_ref[i] - columns[:, 9 + i : 10 + i] for i in range(3)]
            for d in range(3):
                al[d] = sum(columns[:, 3 * i + d : 3 * i + d + 1] * shifted[i] for i in range(3))
        all_of(pbuf.at[p, 0 : NP - 1], p_recv.at[p])
        summed = pbuf[p, 0]
        for i in range(1, NP):
            summed = summed + pbuf[p, i]
        mean_now = summed[0:3, :] / FRAMES

    mean_ref[...] = mean_now
    for d in range(3):
        col[me, :, d * A : (d + 1) * A] = (al[d] - mean_now[d : d + 1, :]).astype(jnp.bfloat16)

    def leg(n, slot):
        rows = pl.ds(n * Q, Q)
        return copy(
            col.at[me, rows], row.at[slot * 2 + k, rows], l_send, l_recv.at[n], (z * 2 + k, leg_z)
        )

    hops = (leg_z - z + NZ) % NZ
    near = jnp.logical_or(hops <= 3, hops >= NZ - 3)

    def leave():
        for n in range(CH):
            leg(n, c).start()

    pl.when(jnp.logical_and(moves, jnp.logical_not(near)))(leave)

    @pl.when(jnp.logical_not(moves))
    def _():
        row[seed * 2 + k] = col[me]

    def chip(oa, ob):
        qa, qb = (pa + oa) % 4, (pb + ob) % 4
        return (qb + k * (qa - qb)) * 4 + qa + k * (qb - qa)

    def at(oa, ob):
        return (chip(oa, ob) * 2 + k, z)

    def part_of(slot, half):
        if half is None:
            return col.at[slot * 2 + k]
        return col.at[slot * 2 + k, half * H : (half + 1) * H]

    HALF = (None, None, 0, 1)
    TOWARD = (1, 3, 1, 3)

    def a_copy(kind, slot):
        r = part_of(slot, HALF[kind])
        return copy(r, r, a_send, a_recv.at[kind], at(TOWARD[kind], 0))

    def b_copy(oa, kind, slot):
        r = part_of(slot, HALF[kind])
        return copy(r, r, b_send, b_recv.at[oa, kind], at(0, TOWARD[kind]))

    def col_sibling(slot, core):
        r = col.at[slot * 2 + core]
        return copy(r, r, cs_send, cs_recv, sibling)

    def have(oa):
        slot = chip(oa, 0)
        b_copy(oa, 0, slot).start()
        b_copy(oa, 1, slot).start()
        col_sibling(slot, k).start()

    def b_pass(oa):
        before, after = chip(oa, 3), chip(oa, 1)
        b_copy(oa, 0, before).wait_recv()
        b_copy(oa, 2, before).start()
        col_sibling(before, k).start()
        b_copy(oa, 1, after).wait_recv()
        b_copy(oa, 3, after).start()
        col_sibling(after, k).start()

    def b_end(oa):
        slot = chip(oa, 2)
        b_copy(oa, 2, slot).wait_recv()
        b_copy(oa, 3, slot).wait_recv()
        col_sibling(slot, k).start()

    right, left = (me, (z + 1) % NZ), (me, (z + NZ - 1) % NZ)

    def off(offset):
        return (seed + offset) % NZ

    def r_copy(way, step, h, slot):
        r = row.at[slot * 2 + k, h * Q : (h + 1) * Q]
        return copy(r, r, r_send, r_recv.at[way, step, h], right if way == 0 else left)

    def row_sibling(offset, core):
        r = row.at[(seeds + 8 * core + offset) % NZ * 2 + core]
        return copy(r, r, rs_send, rs_recv.at[offset], sibling)

    def z_step(s, last=False, between=None):
        slots = off(NZ - s), off(s)
        for h in range(CH):
            for way in range(2):
                r_copy(way, s - 1, h, slots[way]).wait_recv()
                if not last or h // (CH // 2) == way:
                    r_copy(way, s, h, slots[way]).start()
            if between is not None and h < 3:
                between(h)
        row_sibling(NZ - s, k).start()
        row_sibling(s, k).start()

    def product(one, two, i):
        pieces = [(seeds + 8 * core + o) % NZ * 2 + core for o in (one, two) for core in range(2)]
        lanes = pl.ds(pl.multiple_of(i * A + k * 128, 128), 256)
        lhs = jnp.concatenate([row[q, :, lanes] for q in pieces], axis=0)
        rhs = jnp.concatenate([col[q] for q in pieces], axis=0)
        return acc[i] + lax.dot_general(
            lhs, rhs, (((0,), (0,)), ((), ())), preferred_element_type=jnp.float32
        )

    def add(s, i):
        acc[i] = product(NZ - s, s, i)

    def arrived(s):
        row_sibling(s, 1 - k).wait_recv()
        row_sibling(NZ - s, 1 - k).wait_recv()

    def compute(s, _):
        arrived(s)

        def component(i, _):
            add(s, i)
            return 0

        return lax.fori_loop(0, 3, component, 0)

    def finish(i, _):
        total = product(0, NZ // 2, i)
        kept = jnp.where(k == 0, total[0 : A // 2], total[F : F + A // 2]) * (1.0 / FRAMES)
        for d in range(3):
            cov_ref[i, d] = kept[:, d * A : (d + 1) * A]
        return 0

    def step_and_add(s, last=False):
        arrived(s - 2)
        z_step(s, last, lambda i: add(s - 2, i))
        return 0

    a_copy(0, c).start()
    a_copy(1, c).start()
    have(0)
    a_copy(0, chip(3, 0)).wait_recv()
    a_copy(2, chip(3, 0)).start()
    a_copy(1, chip(1, 0)).wait_recv()
    a_copy(3, chip(1, 0)).start()
    pl.when(jnp.logical_and(moves, near))(leave)
    have(3)
    have(1)
    for n in range(CH):

        @pl.when(moves)
        def _():
            leg(n, seed).wait_recv()

        for way in range(2):
            r_copy(way, 0, n, seed).start()
    row_sibling(0, k).start()
    b_pass(0)
    a_copy(2, chip(2, 0)).wait_recv()
    a_copy(3, chip(2, 0)).wait_recv()
    have(2)
    b_pass(3)
    b_pass(1)
    z_step(1)
    b_pass(2)
    z_step(2)
    for oa in (0, 3, 1, 2):
        b_end(oa)

    z_step(3)
    all_of(col.at[0:NZ], cs_recv)
    compute(1, 0)
    lax.fori_loop(4, 7, lambda s, _: step_and_add(s), 0)
    step_and_add(7, last=True)
    lax.fori_loop(6, 8, compute, 0)
    far = off(NZ // 2)
    for p in range(2):
        all_of(zbuf.at[p, 0 : NZ - 1], z_send.at[p])
        all_of(pbuf.at[p, 0 : NP - 1], p_send.at[p])

    @pl.when(moves)
    def _():
        all_of(col.at[0], l_send)

    all_of(col.at[0:3], a_send)
    all_of(col.at[0:12], b_send)
    all_of(col.at[0:NZ], cs_send)
    for h in range(CH):
        r_copy(h // (CH // 2), NZ // 2 - 1, h, far).wait_recv()
    row_sibling(NZ // 2, k).start()
    row_sibling(0, 1 - k).wait_recv()
    row_sibling(NZ // 2, 1 - k).wait_recv()
    lax.fori_loop(0, 3, finish, 0)
    all_of(row.at[0 : NZ - 1], r_send)
    all_of(row.at[0:NZ], rs_send)


def body(frames, reference_structure):
    dma = pltpu.SemaphoreType.DMA
    vmem = pl.BlockSpec(memory_space=pltpu.VMEM)
    hbm = pl.BlockSpec(memory_space=pl.ANY)
    covariance, mean = pl.pallas_call(
        kernel,
        out_shape=(
            jax.ShapeDtypeStruct((3, 3, A // 2, A), jnp.float32),
            jax.ShapeDtypeStruct((3, A), jnp.float32),
        ),
        in_specs=[hbm, hbm],
        out_specs=(vmem, vmem),
        scratch_shapes=[
            pltpu.VMEM((3, F, A), jnp.float32),
            pltpu.VMEM((3, A), jnp.float32),
            pltpu.VMEM((4 * F, A), jnp.float32),
            pltpu.VMEM((16, A), jnp.float32),
            pltpu.VMEM((8, 4 * F), jnp.float32),
            pltpu.VMEM((16, 2 * F), jnp.float32),
            pltpu.VMEM((16, 2 * F), jnp.float32),
            pltpu.VMEM((3, F, A), jnp.float32),
            pltpu.VMEM((2, NZ, 8, 2 * F), jnp.float32),
            pltpu.VMEM((2, NP, 4, A), jnp.float32),
            pltpu.VMEM((NP, F, W), jnp.bfloat16),
            pltpu.VMEM((NP, F, W), jnp.bfloat16),
            pltpu.VMEM((3, 256, W), jnp.float32),
            dma((2,)),
            dma((2,)), dma((2,)), dma((2,)), dma((2,)),
            dma, dma((4,)), dma, dma((4, 4)), dma, dma,
            dma, dma((CH,)), dma, dma((2, 8, CH)), dma, dma((NZ,)),
        ],
        compiler_params=pltpu.CompilerParams(
            collective_id=0, has_side_effects=True, vmem_limit_bytes=44 * 1024 * 1024
        ),
        cost_estimate=pl.CostEstimate(flops=3_000_000_000, bytes_accessed=8_000_000, transcendentals=0),
    )(jnp.transpose(frames, (1, 0, 2)), reference_structure)
    return jnp.transpose(covariance, (0, 2, 1, 3)), mean


def solution(mesh):
    return jax.shard_map(
        body,
        mesh=mesh,
        in_specs=(P("frames", None, "atoms"), P(None, "atoms")),
        out_specs=(P(None, "frames", None, "atoms"), P(None, "atoms")),
        check_vma=False,
    )
```

```python
import jax
import jax.numpy as jnp
from jax import lax
from jax.experimental import pallas as pl
from jax.experimental.pallas import tpu as pltpu
from jax.sharding import PartitionSpec as P

ATOMS = 6144
FRAMES = 2048
POLAR = 8
F = 64
A = 384
W = 3 * A
NZ = 16
NP = 32
H = F // 2
CH = 4
Q = F // CH
MESH = pl.DeviceIdType.MESH
HIGHEST = lax.Precision.HIGHEST


def polar_factor(cross):
    square = sum(cross[i][j] * cross[i][j] for i in range(3) for j in range(3))
    factor = jnp.sqrt(3.0 / square)
    flat = tuple(cross[i][j] * factor for i in range(3) for j in range(3))

    def turn(_, flat):
        e = [flat[0:3], flat[3:6], flat[6:9]]
        cof = [
            [
                e[(i + 1) % 3][(j + 1) % 3] * e[(i + 2) % 3][(j + 2) % 3]
                - e[(i + 1) % 3][(j + 2) % 3] * e[(i + 2) % 3][(j + 1) % 3]
                for j in range(3)
            ]
            for i in range(3)
        ]
        det = e[0][0] * cof[0][0] + e[0][1] * cof[0][1] + e[0][2] * cof[0][2]
        half = 0.5 / det
        return tuple(0.5 * e[i][j] + cof[i][j] * half for i in range(3) for j in range(3))

    flat = lax.fori_loop(0, POLAR, turn, flat)
    return [flat[0:3], flat[3:6], flat[6:9]]


def kernel(
    frames_in, ref_in, cov_ref, mean_ref,
    frames_ref, ref_ref, fa, aug, w, tile, rt, al, zbuf, pbuf, col, row, acc, in_sem,
    z_send, z_recv, p_send, p_recv,
    a_send, a_recv, b_send, b_recv, cs_send, cs_recv,
    l_send, l_recv, r_send, r_recv, rs_send, rs_recv,
):
    me = lax.axis_index("frames")
    z = lax.axis_index("atoms")
    c = me // 2
    k = me % 2
    y = c // 4
    x = c % 4
    pa = x + k * (y - x)
    pb = y + k * (x - y)
    sibling = (c * 2 + 1 - k, z)

    def copy(src, dst, send, recv, device):
        return pltpu.make_async_remote_copy(src, dst, send, recv, device_id=device, device_id_type=MESH)

    def all_of(sized, semaphore):
        pltpu.make_async_copy(sized, sized, semaphore).wait()

    def z_other(i):
        return (z + 8 + ((i + 1) // 2) * (2 * (i % 2) - 1)) % NZ

    def p_other(i):
        return (((y + i // 8 + 2) % 4) * 4 + (x + i // 2 + 2) % 4) * 2 + (k + i) % 2

    def over_z(act):
        def turn(i, _):
            act(i, z_other(i))
            return 0

        lax.fori_loop(0, NZ - 1, turn, 0)

    def over_p(act):
        def turn(i, _):
            act(i, p_other(i))
            return 0

        lax.fori_loop(0, 20, turn, 0)
        lax.fori_loop(21, NP, turn, 0)

    get_frames = pltpu.make_async_copy(frames_in, frames_ref, in_sem.at[0])
    get_ref = pltpu.make_async_copy(ref_in, ref_ref, in_sem.at[1])
    get_frames.start()
    get_ref.start()

    leg_z = (7 * z + c + 8 * k) % NZ
    seeds = (z + 9 * c) % NZ
    seed = (seeds + 8 * k) % NZ
    moves = jnp.logical_or(z != c, leg_z != z)

    barrier = pltpu.get_barrier_semaphore()

    over_z(lambda i, o: pl.semaphore_signal(barrier, inc=1, device_id=(me, o), device_id_type=MESH))
    over_p(lambda i, o: pl.semaphore_signal(barrier, inc=1, device_id=(o, z), device_id_type=MESH))

    get_frames.wait()
    get_ref.wait()
    fa[0:F, :] = frames_ref[0]
    fa[F : 2 * F, :] = frames_ref[2]
    fa[2 * F : 3 * F, :] = frames_ref[1]
    fa[3 * F : 4 * F, :] = jnp.ones((F, A), jnp.float32)
    aug[...] = jnp.zeros((16, A), jnp.float32)
    aug[3:4, :] = jnp.ones((1, A), jnp.float32)
    aug[15:16, :] = jnp.ones((1, A), jnp.float32)
    w[...] = jnp.zeros((8, 4 * F), jnp.float32)
    rt[...] = jnp.zeros((16, 2 * F), jnp.float32)
    acc[...] = jnp.zeros((3, 256, W), jnp.float32)
    low = lax.broadcasted_iota(jnp.int32, (1, 2 * F), 1) < F

    def local_sums():
        nt = (((1,), (1,)), ((), ()))
        first = lax.dot_general(
            aug[0:8, :], fa[0 : 2 * F, :], nt, precision=HIGHEST, preferred_element_type=jnp.float32
        )
        second = lax.dot_general(
            aug[8:16, :], fa[2 * F : 4 * F, :], nt, precision=HIGHEST, preferred_element_type=jnp.float32
        )
        return first + second

    mean_now = ref_ref[...]
    for p in range(2):
        aug[0:3, :] = mean_now
        aug[12:15, :] = mean_now
        zbuf[p, z] = local_sums()
        if p == 0:
            pl.semaphore_wait(barrier, NZ + NP - 2)

        def z_copy(o, slot):
            return copy(zbuf.at[p, slot], zbuf.at[p, slot], z_send.at[p], z_recv.at[p], (me, o))

        over_z(lambda i, o: z_copy(o, z).start())
        all_of(zbuf.at[p, 0 : NZ - 1], z_recv.at[p])
        total = zbuf[p, 0]
        for i in range(1, NZ):
            total = total + zbuf[p, i]
        tile[0:8, :] = total
        tile[8:16, :] = pltpu.roll(total, F, 1)
        centroid = [tile[r : r + 1, :] / ATOMS for r in (3, 7, 11)]
        cross = [
            [tile[4 * i + d : 4 * i + d + 1, :] - centroid[i] * tile[12 + d : 13 + d, :] for d in range(3)]
            for i in range(3)
        ]
        rotation = polar_factor(cross)
        for d in range(3):
            back = -(
                rotation[0][d] * centroid[0] + rotation[1][d] * centroid[1] + rotation[2][d] * centroid[2]
            )
            w[d : d + 1, 0 : 2 * F] = jnp.where(low, rotation[0][d], pltpu.roll(rotation[2][d], F, 1))
            w[d : d + 1, 2 * F : 4 * F] = jnp.where(low, rotation[1][d], pltpu.roll(back, F, 1))
        part = lax.dot_general(
            w[...], fa[...], (((1,), (0,)), ((), ())), precision=HIGHEST, preferred_element_type=jnp.float32
        )
        pbuf[p, me] = part[0:4, :]

        def p_copy(o, slot):
            return copy(pbuf.at[p, slot], pbuf.at[p, slot], p_send.at[p], p_recv.at[p], (o, z))

        over_p(lambda i, o: p_copy(o, me).start())
        if p == 1:
            for i in range(3):
                for d in range(3):
                    rt[3 * i + d : 3 * i + d + 1, :] = rotation[i][d]
                rt[9 + i : 10 + i, :] = centroid[i]
            columns = jnp.transpose(rt[...])[0:F, :]
            shifted = [frames_ref[i] - columns[:, 9 + i : 10 + i] for i in range(3)]
            for d in range(3):
                al[d] = sum(columns[:, 3 * i + d : 3 * i + d + 1] * shifted[i] for i in range(3))
        all_of(pbuf.at[p, 0 : NP - 1], p_recv.at[p])
        summed = pbuf[p, 0]
        for i in range(1, NP):
            summed = summed + pbuf[p, i]
        mean_now = summed[0:3, :] / FRAMES

    mean_ref[...] = mean_now
    for d in range(3):
        col[me, :, d * A : (d + 1) * A] = (al[d] - mean_now[d : d + 1, :]).astype(jnp.bfloat16)

    def leg(n, slot):
        rows = pl.ds(n * Q, Q)
        return copy(
            col.at[me, rows], row.at[slot * 2 + k, rows], l_send, l_recv.at[n], (z * 2 + k, leg_z)
        )

    hops = (leg_z - z + NZ) % NZ
    near = jnp.logical_or(hops <= 3, hops >= NZ - 3)

    def leave():
        for n in range(CH):
            leg(n, c).start()

    pl.when(jnp.logical_and(moves, jnp.logical_not(near)))(leave)

    @pl.when(jnp.logical_not(moves))
    def _():
        row[seed * 2 + k] = col[me]

    def chip(oa, ob):
        qa, qb = (pa + oa) % 4, (pb + ob) % 4
        return (qb + k * (qa - qb)) * 4 + qa + k * (qb - qa)

    def at(oa, ob):
        return (chip(oa, ob) * 2 + k, z)

    def part_of(slot, half):
        if half is None:
            return col.at[slot * 2 + k]
        return col.at[slot * 2 + k, half * H : (half + 1) * H]

    HALF = (None, None, 0, 1)
    TOWARD = (1, 3, 1, 3)

    def a_copy(kind, slot):
        r = part_of(slot, HALF[kind])
        return copy(r, r, a_send, a_recv.at[kind], at(TOWARD[kind], 0))

    def b_copy(oa, kind, slot):
        r = part_of(slot, HALF[kind])
        return copy(r, r, b_send, b_recv.at[oa, kind], at(0, TOWARD[kind]))

    def col_sibling(slot, core):
        r = col.at[slot * 2 + core]
        return copy(r, r, cs_send, cs_recv, sibling)

    def have(oa):
        slot = chip(oa, 0)
        b_copy(oa, 0, slot).start()
        b_copy(oa, 1, slot).start()
        col_sibling(slot, k).start()

    def b_pass(oa):
        before, after = chip(oa, 3), chip(oa, 1)
        b_copy(oa, 0, before).wait_recv()
        b_copy(oa, 2, before).start()
        col_sibling(before, k).start()
        b_copy(oa, 1, after).wait_recv()
        b_copy(oa, 3, after).start()
        col_sibling(after, k).start()

    def b_end(oa):
        slot = chip(oa, 2)
        b_copy(oa, 2, slot).wait_recv()
        b_copy(oa, 3, slot).wait_recv()
        col_sibling(slot, k).start()

    right, left = (me, (z + 1) % NZ), (me, (z + NZ - 1) % NZ)

    def off(offset):
        return (seed + offset) % NZ

    def r_copy(way, step, h, slot):
        r = row.at[slot * 2 + k, h * Q : (h + 1) * Q]
        return copy(r, r, r_send, r_recv.at[way, step, h], right if way == 0 else left)

    def row_sibling(offset, core):
        r = row.at[(seeds + 8 * core + offset) % NZ * 2 + core]
        return copy(r, r, rs_send, rs_recv.at[offset], sibling)

    def z_step(s, last=False, between=None):
        slots = off(NZ - s), off(s)
        for h in range(CH):
            for way in range(2):
                r_copy(way, s - 1, h, slots[way]).wait_recv()
                if not last or h // (CH // 2) == way:
                    r_copy(way, s, h, slots[way]).start()
            if between is not None and h < 3:
                between(h)
        row_sibling(NZ - s, k).start()
        row_sibling(s, k).start()

    def product(one, two, i):
        pieces = [(seeds + 8 * core + o) % NZ * 2 + core for o in (one, two) for core in range(2)]
        lanes = pl.ds(pl.multiple_of(i * A + k * 128, 128), 256)
        lhs = jnp.concatenate([row[q, :, lanes] for q in pieces], axis=0)
        rhs = jnp.concatenate([col[q] for q in pieces], axis=0)
        return acc[i] + lax.dot_general(
            lhs, rhs, (((0,), (0,)), ((), ())), preferred_element_type=jnp.float32
        )

    def add(s, i):
        acc[i] = product(NZ - s, s, i)

    def arrived(s):
        row_sibling(s, 1 - k).wait_recv()
        row_sibling(NZ - s, 1 - k).wait_recv()

    def compute(s, _):
        arrived(s)

        def component(i, _):
            add(s, i)
            return 0

        return lax.fori_loop(0, 3, component, 0)

    def finish(i, _):
        total = product(0, NZ // 2, i)
        kept = jnp.where(k == 0, total[0 : A // 2], total[F : F + A // 2]) * (1.0 / FRAMES)
        for d in range(3):
            cov_ref[i, d] = kept[:, d * A : (d + 1) * A]
        return 0

    def step_and_add(s, last=False):
        arrived(s - 2)
        z_step(s, last, lambda i: add(s - 2, i))
        return 0

    a_copy(0, c).start()
    a_copy(1, c).start()
    have(0)
    a_copy(0, chip(3, 0)).wait_recv()
    a_copy(2, chip(3, 0)).start()
    a_copy(1, chip(1, 0)).wait_recv()
    a_copy(3, chip(1, 0)).start()
    pl.when(jnp.logical_and(moves, near))(leave)
    have(3)
    have(1)
    for n in range(CH):

        @pl.when(moves)
        def _():
            leg(n, seed).wait_recv()

        for way in range(2):
            r_copy(way, 0, n, seed).start()
    row_sibling(0, k).start()
    b_pass(0)
    a_copy(2, chip(2, 0)).wait_recv()
    a_copy(3, chip(2, 0)).wait_recv()
    have(2)
    b_pass(3)
    b_pass(1)
    z_step(1)
    b_pass(2)
    z_step(2)
    for oa in (0, 3, 1, 2):
        b_end(oa)

    z_step(3)
    all_of(col.at[0:NZ], cs_recv)
    compute(1, 0)
    lax.fori_loop(4, 7, lambda s, _: step_and_add(s), 0)
    step_and_add(7, last=True)
    lax.fori_loop(6, 8, compute, 0)
    far = off(NZ // 2)
    for p in range(2):
        all_of(zbuf.at[p, 0 : NZ - 1], z_send.at[p])
        all_of(pbuf.at[p, 0 : NP - 1], p_send.at[p])

    @pl.when(moves)
    def _():
        all_of(col.at[0], l_send)

    all_of(col.at[0:3], a_send)
    all_of(col.at[0:12], b_send)
    all_of(col.at[0:NZ], cs_send)
    for h in range(CH):
        r_copy(h // (CH // 2), NZ // 2 - 1, h, far).wait_recv()
    row_sibling(NZ // 2, k).start()
    row_sibling(0, 1 - k).wait_recv()
    row_sibling(NZ // 2, 1 - k).wait_recv()
    lax.fori_loop(0, 3, finish, 0)
    all_of(row.at[0 : NZ - 1], r_send)
    all_of(row.at[0:NZ], rs_send)


def body(frames, reference_structure):
    dma = pltpu.SemaphoreType.DMA
    vmem = pl.BlockSpec(memory_space=pltpu.VMEM)
    hbm = pl.BlockSpec(memory_space=pl.ANY)
    covariance, mean = pl.pallas_call(
        kernel,
        out_shape=(
            jax.ShapeDtypeStruct((3, 3, A // 2, A), jnp.float32),
            jax.ShapeDtypeStruct((3, A), jnp.float32),
        ),
        in_specs=[hbm, hbm],
        out_specs=(vmem, vmem),
        scratch_shapes=[
            pltpu.VMEM((3, F, A), jnp.float32),
            pltpu.VMEM((3, A), jnp.float32),
            pltpu.VMEM((4 * F, A), jnp.float32),
            pltpu.VMEM((16, A), jnp.float32),
            pltpu.VMEM((8, 4 * F), jnp.float32),
            pltpu.VMEM((16, 2 * F), jnp.float32),
            pltpu.VMEM((16, 2 * F), jnp.float32),
            pltpu.VMEM((3, F, A), jnp.float32),
            pltpu.VMEM((2, NZ, 8, 2 * F), jnp.float32),
            pltpu.VMEM((2, NP, 4, A), jnp.float32),
            pltpu.VMEM((NP, F, W), jnp.bfloat16),
            pltpu.VMEM((NP, F, W), jnp.bfloat16),
            pltpu.VMEM((3, 256, W), jnp.float32),
            dma((2,)),
            dma((2,)), dma((2,)), dma((2,)), dma((2,)),
            dma, dma((4,)), dma, dma((4, 4)), dma, dma,
            dma, dma((CH,)), dma, dma((2, 8, CH)), dma, dma((NZ,)),
        ],
        compiler_params=pltpu.CompilerParams(
            collective_id=0, has_side_effects=True, vmem_limit_bytes=44 * 1024 * 1024
        ),
        cost_estimate=pl.CostEstimate(flops=3_000_000_000, bytes_accessed=8_000_000, transcendentals=0),
    )(jnp.transpose(frames, (1, 0, 2)), reference_structure)
    return jnp.transpose(covariance, (0, 2, 1, 3)), mean


def solution(mesh):
    return jax.shard_map(
        body,
        mesh=mesh,
        in_specs=(P("frames", None, "atoms"), P(None, "atoms")),
        out_specs=(P(None, "frames", None, "atoms"), P(None, "atoms")),
        check_vma=False,
    )
```

```python
import jax
import jax.numpy as jnp
from jax import lax
from jax.experimental import pallas as pl
from jax.experimental.pallas import tpu as pltpu
from jax.sharding import PartitionSpec as P

ATOMS = 6144
FRAMES = 2048
POLAR = 8
F = 64
A = 384
W = 3 * A
NZ = 16
NP = 32
H = F // 2
CH = 4
Q = F // CH
MESH = pl.DeviceIdType.MESH
HIGHEST = lax.Precision.HIGHEST


def polar_factor(cross):
    square = sum(cross[i][j] * cross[i][j] for i in range(3) for j in range(3))
    factor = jnp.sqrt(3.0 / square)
    flat = tuple(cross[i][j] * factor for i in range(3) for j in range(3))

    def turn(_, flat):
        e = [flat[0:3], flat[3:6], flat[6:9]]
        cof = [
            [
                e[(i + 1) % 3][(j + 1) % 3] * e[(i + 2) % 3][(j + 2) % 3]
                - e[(i + 1) % 3][(j + 2) % 3] * e[(i + 2) % 3][(j + 1) % 3]
                for j in range(3)
            ]
            for i in range(3)
        ]
        det = e[0][0] * cof[0][0] + e[0][1] * cof[0][1] + e[0][2] * cof[0][2]
        half = 0.5 / det
        return tuple(0.5 * e[i][j] + cof[i][j] * half for i in range(3) for j in range(3))

    flat = lax.fori_loop(0, POLAR, turn, flat)
    return [flat[0:3], flat[3:6], flat[6:9]]


def kernel(
    frames_in, ref_in, cov_ref, mean_ref,
    frames_ref, ref_ref, fa, aug, w, tile, rt, al, zbuf, pbuf, col, row, acc, in_sem,
    z_send, z_recv, p_send, p_recv,
    a_send, a_recv, b_send, b_recv, cs_send, cs_recv,
    l_send, l_recv, r_send, r_recv, rs_send, rs_recv,
):
    me = lax.axis_index("frames")
    z = lax.axis_index("atoms")
    c = me // 2
    k = me % 2
    y = c // 4
    x = c % 4
    pa = x + k * (y - x)
    pb = y + k * (x - y)
    sibling = (c * 2 + 1 - k, z)

    def copy(src, dst, send, recv, device):
        return pltpu.make_async_remote_copy(src, dst, send, recv, device_id=device, device_id_type=MESH)

    def all_of(sized, semaphore):
        pltpu.make_async_copy(sized, sized, semaphore).wait()

    def z_other(i):
        return (z + 8 + ((i + 1) // 2) * (2 * (i % 2) - 1)) % NZ

    def p_other(i):
        return (((y + i // 8 + 2) % 4) * 4 + (x + i // 2 + 2) % 4) * 2 + (k + i) % 2

    def over_z(act):
        def turn(i, _):
            act(i, z_other(i))
            return 0

        lax.fori_loop(0, NZ - 1, turn, 0)

    def over_p(act):
        def turn(i, _):
            act(i, p_other(i))
            return 0

        lax.fori_loop(0, 20, turn, 0)
        lax.fori_loop(21, NP, turn, 0)

    get_frames = pltpu.make_async_copy(frames_in, frames_ref, in_sem.at[0])
    get_ref = pltpu.make_async_copy(ref_in, ref_ref, in_sem.at[1])
    get_frames.start()
    get_ref.start()

    leg_z = (7 * z + c + 8 * k) % NZ
    seeds = (z + 9 * c) % NZ
    seed = (seeds + 8 * k) % NZ
    moves = jnp.logical_or(z != c, leg_z != z)

    barrier = pltpu.get_barrier_semaphore()

    @pl.when(moves)
    def _():
        pl.semaphore_signal(barrier, inc=1, device_id=(seed * 2 + k, c), device_id_type=MESH)

    over_z(lambda i, o: pl.semaphore_signal(barrier, inc=1, device_id=(me, o), device_id_type=MESH))
    over_p(lambda i, o: pl.semaphore_signal(barrier, inc=1, device_id=(o, z), device_id_type=MESH))

    get_frames.wait()
    get_ref.wait()
    fa[0:F, :] = frames_ref[0]
    fa[F : 2 * F, :] = frames_ref[2]
    fa[2 * F : 3 * F, :] = frames_ref[1]
    fa[3 * F : 4 * F, :] = jnp.ones((F, A), jnp.float32)
    aug[...] = jnp.zeros((16, A), jnp.float32)
    aug[3:4, :] = jnp.ones((1, A), jnp.float32)
    aug[15:16, :] = jnp.ones((1, A), jnp.float32)
    w[...] = jnp.zeros((8, 4 * F), jnp.float32)
    rt[...] = jnp.zeros((16, 2 * F), jnp.float32)
    acc[...] = jnp.zeros((3, 256, W), jnp.float32)
    low = lax.broadcasted_iota(jnp.int32, (1, 2 * F), 1) < F

    def local_sums():
        nt = (((1,), (1,)), ((), ()))
        first = lax.dot_general(
            aug[0:8, :], fa[0 : 2 * F, :], nt, precision=HIGHEST, preferred_element_type=jnp.float32
        )
        second = lax.dot_general(
            aug[8:16, :], fa[2 * F : 4 * F, :], nt, precision=HIGHEST, preferred_element_type=jnp.float32
        )
        return first + second

    mean_now = ref_ref[...]
    for p in range(2):
        aug[0:3, :] = mean_now
        aug[12:15, :] = mean_now
        zbuf[p, z] = local_sums()
        if p == 0:
            pl.semaphore_wait(barrier, NZ + NP - 2 + jnp.where(moves, 1, 0))

        def z_copy(o, slot):
            return copy(zbuf.at[p, slot], zbuf.at[p, slot], z_send.at[p], z_recv.at[p], (me, o))

        over_z(lambda i, o: z_copy(o, z).start())
        all_of(zbuf.at[p, 0 : NZ - 1], z_recv.at[p])
        total = zbuf[p, 0]
        for i in range(1, NZ):
            total = total + zbuf[p, i]
        tile[0:8, :] = total
        tile[8:16, :] = pltpu.roll(total, F, 1)
        centroid = [tile[r : r + 1, :] / ATOMS for r in (3, 7, 11)]
        cross = [
            [tile[4 * i + d : 4 * i + d + 1, :] - centroid[i] * tile[12 + d : 13 + d, :] for d in range(3)]
            for i in range(3)
        ]
        rotation = polar_factor(cross)
        for d in range(3):
            back = -(
                rotation[0][d] * centroid[0] + rotation[1][d] * centroid[1] + rotation[2][d] * centroid[2]
            )
            w[d : d + 1, 0 : 2 * F] = jnp.where(low, rotation[0][d], pltpu.roll(rotation[2][d], F, 1))
            w[d : d + 1, 2 * F : 4 * F] = jnp.where(low, rotation[1][d], pltpu.roll(back, F, 1))
        part = lax.dot_general(
            w[...], fa[...], (((1,), (0,)), ((), ())), precision=HIGHEST, preferred_element_type=jnp.float32
        )
        pbuf[p, me] = part[0:4, :]

        def p_copy(o, slot):
            return copy(pbuf.at[p, slot], pbuf.at[p, slot], p_send.at[p], p_recv.at[p], (o, z))

        over_p(lambda i, o: p_copy(o, me).start())
        if p == 1:
            for i in range(3):
                for d in range(3):
                    rt[3 * i + d : 3 * i + d + 1, :] = rotation[i][d]
                rt[9 + i : 10 + i, :] = centroid[i]
            columns = jnp.transpose(rt[...])[0:F, :]
            shifted = [frames_ref[i] - columns[:, 9 + i : 10 + i] for i in range(3)]
            for d in range(3):
                al[d] = sum(columns[:, 3 * i + d : 3 * i + d + 1] * shifted[i] for i in range(3))
        all_of(pbuf.at[p, 0 : NP - 1], p_recv.at[p])
        summed = pbuf[p, 0]
        for i in range(1, NP):
            summed = summed + pbuf[p, i]
        mean_now = summed[0:3, :] / FRAMES

    mean_ref[...] = mean_now
    for d in range(3):
        col[me, :, d * A : (d + 1) * A] = (al[d] - mean_now[d : d + 1, :]).astype(jnp.bfloat16)

    def leg(n, slot):
        rows = pl.ds(n * Q, Q)
        return copy(
            col.at[me, rows], row.at[slot * 2 + k, rows], l_send, l_recv.at[n], (z * 2 + k, leg_z)
        )

    hops = (leg_z - z + NZ) % NZ
    near = jnp.logical_or(hops <= 3, hops >= NZ - 3)

    def leave():
        for n in range(CH):
            leg(n, c).start()

    pl.when(jnp.logical_and(moves, jnp.logical_not(near)))(leave)

    @pl.when(jnp.logical_not(moves))
    def _():
        row[seed * 2 + k] = col[me]

    def chip(oa, ob):
        qa, qb = (pa + oa) % 4, (pb + ob) % 4
        return (qb + k * (qa - qb)) * 4 + qa + k * (qb - qa)

    def at(oa, ob):
        return (chip(oa, ob) * 2 + k, z)

    def part_of(slot, half):
        if half is None:
            return col.at[slot * 2 + k]
        return col.at[slot * 2 + k, half * H : (half + 1) * H]

    HALF = (None, None, 0, 1)
    TOWARD = (1, 3, 1, 3)

    def a_copy(kind, slot):
        r = part_of(slot, HALF[kind])
        return copy(r, r, a_send, a_recv.at[kind], at(TOWARD[kind], 0))

    def b_copy(oa, kind, slot):
        r = part_of(slot, HALF[kind])
        return copy(r, r, b_send, b_recv.at[oa, kind], at(0, TOWARD[kind]))

    def col_sibling(slot, core):
        r = col.at[slot * 2 + core]
        return copy(r, r, cs_send, cs_recv, sibling)

    def have(oa):
        slot = chip(oa, 0)
        b_copy(oa, 0, slot).start()
        b_copy(oa, 1, slot).start()
        col_sibling(slot, k).start()

    def b_pass(oa):
        before, after = chip(oa, 3), chip(oa, 1)
        b_copy(oa, 0, before).wait_recv()
        b_copy(oa, 2, before).start()
        col_sibling(before, k).start()
        b_copy(oa, 1, after).wait_recv()
        b_copy(oa, 3, after).start()
        col_sibling(after, k).start()

    def b_end(oa):
        slot = chip(oa, 2)
        b_copy(oa, 2, slot).wait_recv()
        b_copy(oa, 3, slot).wait_recv()
        col_sibling(slot, k).start()

    right, left = (me, (z + 1) % NZ), (me, (z + NZ - 1) % NZ)

    def off(offset):
        return (seed + offset) % NZ

    def r_copy(way, step, h, slot):
        r = row.at[slot * 2 + k, h * Q : (h + 1) * Q]
        return copy(r, r, r_send, r_recv.at[way, step, h], right if way == 0 else left)

    def row_sibling(offset, core):
        r = row.at[(seeds + 8 * core + offset) % NZ * 2 + core]
        return copy(r, r, rs_send, rs_recv.at[offset], sibling)

    def z_step(s, last=False, between=None):
        slots = off(NZ - s), off(s)
        for h in range(CH):
            for way in range(2):
                r_copy(way, s - 1, h, slots[way]).wait_recv()
                if not last or h // (CH // 2) == way:
                    r_copy(way, s, h, slots[way]).start()
            if between is not None and h < 3:
                between(h)
        row_sibling(NZ - s, k).start()
        row_sibling(s, k).start()

    def product(offsets, i):
        pieces = [(seeds + 8 * core + o) % NZ * 2 + core for o in offsets for core in range(2)]
        lanes = pl.ds(pl.multiple_of(i * A + k * 128, 128), 256)
        lhs = jnp.concatenate([row[q, :, lanes] for q in pieces], axis=0)
        rhs = jnp.concatenate([col[q] for q in pieces], axis=0)
        return acc[i] + lax.dot_general(
            lhs, rhs, (((0,), (0,)), ((), ())), preferred_element_type=jnp.float32
        )

    def add(s, i):
        acc[i] = product((NZ - s, s), i)

    def arrived(s):
        row_sibling(s, 1 - k).wait_recv()
        row_sibling(NZ - s, 1 - k).wait_recv()

    def compute(s, _):
        arrived(s)

        def component(i, _):
            add(s, i)
            return 0

        return lax.fori_loop(0, 3, component, 0)

    def add_seeds(i, _):
        acc[i] = product((0,), i)
        return 0

    def finish(i, _):
        total = product((NZ // 2,), i)
        kept = jnp.where(k == 0, total[0 : A // 2], total[F : F + A // 2]) * (1.0 / FRAMES)
        for d in range(3):
            cov_ref[i, d] = kept[:, d * A : (d + 1) * A]
        return 0

    def step_and_add(s, last=False):
        arrived(s - 2)
        z_step(s, last, lambda i: add(s - 2, i))
        return 0

    a_copy(0, c).start()
    a_copy(1, c).start()
    have(0)
    a_copy(0, chip(3, 0)).wait_recv()
    a_copy(2, chip(3, 0)).start()
    a_copy(1, chip(1, 0)).wait_recv()
    a_copy(3, chip(1, 0)).start()
    pl.when(jnp.logical_and(moves, near))(leave)
    have(3)
    have(1)
    for n in range(CH):

        @pl.when(moves)
        def _():
            leg(n, seed).wait_recv()

        for way in range(2):
            r_copy(way, 0, n, seed).start()
    row_sibling(0, k).start()
    b_pass(0)
    a_copy(2, chip(2, 0)).wait_recv()
    a_copy(3, chip(2, 0)).wait_recv()
    have(2)
    b_pass(3)
    b_pass(1)
    z_step(1)
    b_pass(2)
    z_step(2)
    for oa in (0, 3, 1, 2):
        b_end(oa)

    z_step(3)
    all_of(col.at[0:NZ], cs_recv)
    compute(1, 0)
    lax.fori_loop(4, 7, lambda s, _: step_and_add(s), 0)
    step_and_add(7, last=True)
    lax.fori_loop(6, 7, compute, 0)
    row_sibling(0, 1 - k).wait_recv()
    lax.fori_loop(0, 3, add_seeds, 0)
    compute(7, 0)
    far = off(NZ // 2)
    for p in range(2):
        all_of(zbuf.at[p, 0 : NZ - 1], z_send.at[p])
        all_of(pbuf.at[p, 0 : NP - 1], p_send.at[p])

    @pl.when(moves)
    def _():
        all_of(col.at[0], l_send)

    all_of(col.at[0:3], a_send)
    all_of(col.at[0:12], b_send)
    all_of(col.at[0:NZ], cs_send)
    for h in range(CH):
        r_copy(h // (CH // 2), NZ // 2 - 1, h, far).wait_recv()
    row_sibling(NZ // 2, k).start()
    row_sibling(NZ // 2, 1 - k).wait_recv()
    lax.fori_loop(0, 3, finish, 0)
    all_of(row.at[0 : NZ - 1], r_send)
    all_of(row.at[0:NZ], rs_send)


def body(frames, reference_structure):
    dma = pltpu.SemaphoreType.DMA
    vmem = pl.BlockSpec(memory_space=pltpu.VMEM)
    hbm = pl.BlockSpec(memory_space=pl.ANY)
    covariance, mean = pl.pallas_call(
        kernel,
        out_shape=(
            jax.ShapeDtypeStruct((3, 3, A // 2, A), jnp.float32),
            jax.ShapeDtypeStruct((3, A), jnp.float32),
        ),
        in_specs=[hbm, hbm],
        out_specs=(vmem, vmem),
        scratch_shapes=[
            pltpu.VMEM((3, F, A), jnp.float32),
            pltpu.VMEM((3, A), jnp.float32),
            pltpu.VMEM((4 * F, A), jnp.float32),
            pltpu.VMEM((16, A), jnp.float32),
            pltpu.VMEM((8, 4 * F), jnp.float32),
            pltpu.VMEM((16, 2 * F), jnp.float32),
            pltpu.VMEM((16, 2 * F), jnp.float32),
            pltpu.VMEM((3, F, A), jnp.float32),
            pltpu.VMEM((2, NZ, 8, 2 * F), jnp.float32),
            pltpu.VMEM((2, NP, 4, A), jnp.float32),
            pltpu.VMEM((NP, F, W), jnp.bfloat16),
            pltpu.VMEM((NP, F, W), jnp.bfloat16),
            pltpu.VMEM((3, 256, W), jnp.float32),
            dma((2,)),
            dma((2,)), dma((2,)), dma((2,)), dma((2,)),
            dma, dma((4,)), dma, dma((4, 4)), dma, dma,
            dma, dma((CH,)), dma, dma((2, 8, CH)), dma, dma((NZ,)),
        ],
        compiler_params=pltpu.CompilerParams(
            collective_id=0, has_side_effects=True, vmem_limit_bytes=44 * 1024 * 1024
        ),
        cost_estimate=pl.CostEstimate(flops=3_000_000_000, bytes_accessed=8_000_000, transcendentals=0),
    )(jnp.transpose(frames, (1, 0, 2)), reference_structure)
    return jnp.transpose(covariance, (0, 2, 1, 3)), mean


def solution(mesh):
    return jax.shard_map(
        body,
        mesh=mesh,
        in_specs=(P("frames", None, "atoms"), P(None, "atoms")),
        out_specs=(P(None, "frames", None, "atoms"), P(None, "atoms")),
        check_vma=False,
    )
```
